512 devices in a mesh: vis: 64 (over z, x, core), txt: 8 (over y).
Axes of the slice: x: 4, y: 8, z: 8, core: 2. Of those that a mesh axis runs over, the one named last changes fastest.
Arguments:
- queries: bfloat16 [65536, 4096], P(('txt', 'vis')), may hold values from -6 to 6
- out_grad: bfloat16 [65536, 4096], P(('txt', 'vis')), may hold values from -6 to 6
- vision: bfloat16 [8, 384, 8192], P('txt', None, 'vis'), may hold values from -6 to 6
- w_kv: bfloat16 [8192, 1024], P('vis', 'txt'), may hold values from -1 to 1
- links: int32 [8, 64, 16], P('txt'), may hold values from 0 to 1, as said below
- img_count: int32 [8], P('txt'), may hold values from 1 to 16, as said below
Outputs:
- query_grad: bfloat16 [65536, 4096], P(('txt', 'vis'))
- vision_grad: bfloat16 [8, 384, 8192], P('txt', None, 'vis')
- w_kv_grad: float32 [8192, 1024], P('vis', 'txt')
The draws below stay inside these ranges and needn't reach their ends.
Inputs may be any that keep to these rules, and one draw needn't show every extreme that they name: `links`: entries are 0 or 1; every block is linked to slot 0. `img_count`: slots at or past a document's count are not seen, whatever links says.
All inputs are finite; a program needn't handle non-finite values.
Results may differ from the reference program's by a relative error of at most 0.025.
Values may be sent and summed in bfloat16 or wider, within the bound.
A program may use at most 64 MiB of HBM per device.

```python
import jax
import jax.numpy as jnp

D = 8192
HD = 128
QH = 32
KVH = 4
IMG_DOC = 16
IMG_LEN = 24
BLOCK = 128
DOCS = 8
TEXT = 65536
NB = 64
DOC_TOK = 384
QW = 4096
KVW = 512


def head_signs(key):
    bits = jax.random.bernoulli(jax.random.fold_in(key, 101), 0.5, (KVH, HD))
    return jnp.where(bits, 1.0, -1.0).astype(jnp.float32)


def draw_queries(key, part):
    signs = head_signs(key)
    key = jax.random.fold_in(key, 3)
    base_key, power_key = jax.random.split(key)
    base = jnp.clip(jax.random.normal(base_key, (TEXT, QW), jnp.float32), -6.0, 6.0)
    strength = jax.random.uniform(power_key, (TEXT, QH), jnp.float32, 2.5, 6.0)
    query_signs = jnp.repeat(signs, QH // KVH, axis=0)
    planted = (strength[:, :, None] * query_signs[None, :, :]).reshape(TEXT, QW)
    chosen = jnp.arange(TEXT, dtype=jnp.int32) % 128 == 7
    return jnp.where(chosen[:, None], planted, base).astype(jnp.bfloat16)


def draw_w_kv(key, part):
    signs = head_signs(key)
    key = jax.random.fold_in(key, 5)
    base = jnp.clip(jax.random.normal(key, (D, 2 * KVW), jnp.float32), -6.0, 6.0) * D ** (-0.5)
    level = 0.03125
    key_row = jnp.concatenate([signs.reshape(KVW) * level, jnp.zeros((KVW,), jnp.float32)])
    rows = jnp.arange(D, dtype=jnp.int32) < 32
    columns = jnp.arange(2 * KVW, dtype=jnp.int32) < KVW
    chosen = rows[:, None] & columns[None, :]
    return jnp.where(chosen, key_row[None, :], base).astype(jnp.bfloat16)


def draw_vision(key, part):
    key = jax.random.fold_in(key, 9)
    base = jnp.clip(jax.random.normal(key, (DOCS, DOC_TOK, D), jnp.float32), -6.0, 6.0)
    features = jnp.arange(D, dtype=jnp.int32)
    first = jnp.where(features < 16, 6.0, 0.0).astype(jnp.float32)
    second = jnp.where((features >= 16) & (features < 32), 5.9375, 0.0).astype(jnp.float32)
    tokens = jnp.arange(DOC_TOK, dtype=jnp.int32)
    planted = jnp.where((tokens == 0)[:, None], first[None, :], second[None, :])
    chosen = (tokens < 2)[None, :, None]
    return jnp.where(chosen, planted[None, :, :], base).astype(jnp.bfloat16)


def draw_links(key, part):
    key = jax.random.fold_in(key, 7)
    linked = jax.random.randint(key, (DOCS, NB, IMG_DOC), 0, 2)
    linked = linked.at[:, :, 0].set(1)
    return linked.astype(jnp.int32)


def draw_img_count(key, part):
    key = jax.random.fold_in(key, 11)
    count_key, full_key, small_key, step_key = jax.random.split(key, 4)
    counted = jax.random.randint(count_key, (DOCS,), 1, IMG_DOC + 1)
    full_doc = jax.random.randint(full_key, (), 0, DOCS)
    small_doc = (full_doc + jax.random.randint(step_key, (), 1, DOCS)) % DOCS
    small_value = jax.random.randint(small_key, (), 1, 5)
    counted = counted.at[small_doc].set(small_value)
    counted = counted.at[full_doc].set(IMG_DOC)
    return counted.astype(jnp.int32)


def block_scale(rng, shape, cuts, least, largest):
    loudness, own = 1.0, jax.random.fold_in(rng, 6)
    for position, blocks in cuts:
        heights = jnp.exp(jax.random.uniform(jax.random.fold_in(own, position), (blocks,), jnp.float32, least / len(cuts), largest / len(cuts)))
        loudness = loudness * jnp.repeat(heights, shape[position] // blocks).reshape([-1 if axis == position else 1 for axis in range(len(shape))])
    return loudness


def normal_values(key, extent, deviation, reach, cuts=(), held_as=jnp.bfloat16):
    level = block_scale(key, extent, cuts, -0.22, 0.18) if cuts else 1.0
    drawn = jax.random.normal(key, extent, jnp.float32) * deviation * level
    return jnp.minimum(jnp.maximum(drawn, -reach), reach).astype(held_as)


def setup_inputs(seed: int = 0) -> dict:
    streams_of = jax.random.split(jax.random.key(seed), 7)
    queries = draw_queries(jax.random.fold_in(streams_of[6], 71), 0)
    out_grad = normal_values(streams_of[1], (TEXT, QW), 1.0, 6.0, ((0, 512),))
    vision = draw_vision(jax.random.fold_in(streams_of[6], 71), 0)
    w_kv = draw_w_kv(jax.random.fold_in(streams_of[6], 71), 0)
    links = draw_links(jax.random.fold_in(streams_of[6], 71), 0)
    img_count = draw_img_count(jax.random.fold_in(streams_of[6], 71), 0)
    return {"queries": queries, "out_grad": out_grad, "vision": vision, "w_kv": w_kv, "links": links, "img_count": img_count}


def reference(queries, out_grad, vision, w_kv, links, img_count):
    kv_width = KVH * HD
    group_size = QH // KVH
    scaling = HD ** -0.5
    seg_rows = queries.shape[0] // DOCS
    grad_parts = []
    vision_parts = []
    weight_total = jnp.zeros(w_kv.shape, jnp.float32)
    for doc_index in range(DOCS):
        images = vision[doc_index]
        kv_pair = jnp.dot(images, w_kv, preferred_element_type=jnp.float32).astype(jnp.bfloat16)
        block_ids = (jnp.arange(seg_rows, dtype=jnp.int32) // BLOCK).astype(jnp.int32)
        link_rows = jnp.take(links[doc_index], block_ids, axis=0)
        image_ids = jnp.arange(IMG_DOC, dtype=jnp.int32)
        live_links = (link_rows == 1) & (image_ids[None, :] < img_count[doc_index])
        allowed = jnp.repeat(live_links, IMG_LEN, axis=1)
        query_doc = queries[doc_index * seg_rows:(doc_index + 1) * seg_rows]
        grad_doc = out_grad[doc_index * seg_rows:(doc_index + 1) * seg_rows]
        dq_parts = []
        key_parts = []
        value_parts = []
        for head_index in range(KVH):
            low = head_index * group_size * HD
            high = (head_index + 1) * group_size * HD
            query_head = query_doc[:, low:high].reshape(seg_rows, group_size, HD).astype(jnp.float32)
            grad_head = grad_doc[:, low:high].reshape(seg_rows, group_size, HD).astype(jnp.float32)
            key_head = kv_pair[:, head_index * HD:(head_index + 1) * HD].astype(jnp.float32)
            value_head = kv_pair[:, kv_width + head_index * HD:kv_width + (head_index + 1) * HD].astype(jnp.float32)
            scores = jnp.einsum("rgd,td->rgt", query_head, key_head) * scaling
            scores = jnp.where(allowed[:, None, :], scores, -1e30)
            row_max = jnp.max(scores, axis=-1, keepdims=True)
            exp_scores = jnp.exp(scores - row_max)
            probs = exp_scores / jnp.sum(exp_scores, axis=-1, keepdims=True)
            prob_grad = jnp.einsum("rgd,td->rgt", grad_head, value_head)
            row_delta = jnp.sum(probs * prob_grad, axis=-1, keepdims=True)
            score_grad = (probs * (prob_grad - row_delta)).astype(jnp.bfloat16).astype(jnp.float32)
            probs_b = probs.astype(jnp.bfloat16).astype(jnp.float32)
            dq_head = jnp.einsum("rgt,td->rgd", score_grad, key_head) * scaling
            dq_parts.append(dq_head.reshape(seg_rows, group_size * HD).astype(jnp.bfloat16))
            key_parts.append(jnp.einsum("rgt,rgd->td", score_grad, query_head) * scaling)
            value_parts.append(jnp.einsum("rgt,rgd->td", probs_b, grad_head))
        grad_parts.append(jnp.concatenate(dq_parts, axis=1))
        kv_grad = jnp.concatenate(key_parts + value_parts, axis=1).astype(jnp.bfloat16)
        vision_parts.append(jnp.dot(kv_grad, w_kv.T, preferred_element_type=jnp.float32).astype(jnp.bfloat16))
        weight_total = weight_total + jnp.dot(images.T, kv_grad, preferred_element_type=jnp.float32)
    return jnp.concatenate(grad_parts, axis=0), jnp.stack(vision_parts, axis=0), weight_total
```

```python
import jax
import jax.numpy as jnp
from jax import lax
from jax.experimental import pallas as pl
from jax.experimental.pallas import tpu as pltpu
from jax.sharding import PartitionSpec as P

HD = 128
QH = 32
KVH = 4
GROUP = QH // KVH
IMG_DOC = 16
IMG_LEN = 24
TOK = IMG_DOC * IMG_LEN
NZ, NX, NY = 8, 4, 8
PIECE = TOK // NZ
SCALE = HD ** (-0.5)
LOG2E = 1.4426950408889634
MESH = pl.DeviceIdType.MESH
F32, BF16 = jnp.float32, jnp.bfloat16

CORE, XS, ZS, AZ, AX, AC = 0, 4, 8, 16, 24, 28
FWD, BWD, WG, YS = 0, 32, 64, 72
SEMS = 80


def near_first(n):
    return sorted(range(1, n), key=lambda k: min(k, n - k))


def far_first(n):
    return near_first(n)[::-1]


def body(
    q_hbm, do_hbm, vision_ref, w_ref, links_ref, count_ref,
    dq_hbm, vg_ref, wg_ref,
    q_ref, do_ref, dq_ref, bias_ref, vt_ref, kt_ref, w_all,
    p_ref, sg_ref, grads,
    own1, csend1, crecv1, xsend1, xrecv1, xown1, zsend1, zrecv1, kv1,
    own2, csend2, crecv2, xsend2, xrecv2, xown2, zsend2, zrecv2, kv2,
    ysend, yrecv, yown,
    ssem, rsem, lsem,
):
    v = lax.axis_index("vis")
    t = lax.axis_index("txt")
    core = lax.rem(v, 2)
    x = lax.rem(lax.div(v, 2), NX)
    z = lax.div(v, 2 * NX)
    other = 1 - core
    mine = core * KVH + x

    def vis_at(zz, xx, cc):
        return (zz * NX + xx) * 2 + cc

    partner = (vis_at(z, x, other), t)

    def x_dev(k):
        return (vis_at(z, lax.rem(x + k, NX), core), t)

    def z_dev(k):
        return (vis_at(lax.rem(z + k, NZ), x, core), t)

    def y_dev(k):
        return (v, lax.rem(t + k, NY))

    def piece(zz):
        return pl.ds(pl.multiple_of(zz * PIECE, PIECE), PIECE)

    def link(src, dst, sem, dev):
        return pltpu.make_async_remote_copy(
            src_ref=src, dst_ref=dst, send_sem=ssem.at[sem], recv_sem=rsem.at[sem],
            device_id=dev, device_id_type=MESH,
        )

    q_in = pltpu.make_async_copy(q_hbm, q_ref, lsem.at[0])
    do_in = pltpu.make_async_copy(do_hbm, do_ref, lsem.at[1])
    q_in.start()
    do_in.start()

    barrier = pltpu.get_barrier_semaphore()
    partners = (
        [partner]
        + [x_dev(k) for k in range(1, NX)]
        + [z_dev(k) for k in range(1, NZ)]
        + [y_dev(k) for k in range(1, NY)]
    )
    for dev in partners:
        pl.semaphore_signal(barrier, inc=1, device_id=dev, device_id_type=MESH)
    pl.semaphore_wait(barrier, len(partners))

    def w_copy(k):
        return link(w_ref, w_all.at[t], WG + k, y_dev(k))

    for k in far_first(NY):
        w_copy(k).start()
    w_all[t] = w_ref[...]

    block = lax.broadcasted_iota(jnp.int32, links_ref.shape[1:], 1)
    slot = lax.broadcasted_iota(jnp.int32, (IMG_DOC, 1), 0)
    linked = jnp.sum(jnp.where(block == v, links_ref[0], 0), axis=1, keepdims=True)
    bias = jnp.where((linked == 1) & (slot < count_ref[0]), 0.0, -1e30)
    for s in range(IMG_DOC):
        bias_ref[s * IMG_LEN : (s + 1) * IMG_LEN, :] = jnp.broadcast_to(
            bias[s : s + 1, :], (IMG_LEN, HD)
        )
    vt_ref[...] = vision_ref[0].T

    class Sums:
        def __init__(self, base, own, csend, crecv, xsend, xrecv, xown, zsend, zrecv, kv):
            self.base, self.own, self.csend, self.crecv = base, own, csend, crecv
            self.xsend, self.xrecv, self.xown = xsend, xrecv, xown
            self.zsend, self.zrecv, self.kv = zsend, zrecv, kv

        def core_copy(self, h):
            return link(self.csend.at[h], self.crecv.at[h], self.base + CORE + h, partner)

        def x_copy(self, k):
            return link(self.xsend.at[k], self.xrecv.at[k], self.base + XS + k, x_dev(k))

        def z_copy(self, k):
            rows = piece(lax.rem(z + k, NZ))
            return link(self.zsend.at[rows, :], self.zrecv.at[k], self.base + ZS + k, z_dev(k))

        def az_copy(self, k, zz):
            ref = self.kv.at[mine, piece(zz), :]
            return link(ref, ref, self.base + AZ + k, z_dev(k))

        def ax_copy(self, k, h):
            ref = self.kv.at[core * KVH + h]
            return link(ref, ref, self.base + AX + k, x_dev(k))

        def ac_copy(self, kind, h):
            ref = self.kv.at[kind * KVH + h]
            return link(ref, ref, self.base + AC + h, partner)

        def x_step(self, h):
            self.core_copy(h).wait_recv()
            total = self.own[h] + self.crecv[h].astype(F32)
            k = lax.rem(h - x + NX, NX)

            @pl.when(k == 0)
            def _():
                self.xown[...] = total

            @pl.when(k != 0)
            def _():
                self.xsend[k] = total.astype(BF16)
                self.x_copy(k).start()

        def z_stage(self):
            total = self.xown[...]
            for k in near_first(NX):
                self.x_copy(k).wait_recv()
                total = total + self.xrecv[k].astype(F32)
            self.xown[...] = total
            self.zsend[...] = total.astype(BF16)
            for k in far_first(NZ):
                self.z_copy(k).start()
            part = self.xown[piece(z), :]
            for k in near_first(NZ):
                self.z_copy(k).wait_recv()
                part = part + self.zrecv[k].astype(F32)
            self.kv[mine, piece(z), :] = part.astype(BF16)
            for k in far_first(NZ):
                self.az_copy(k, z).start()
            for k in near_first(NZ):
                self.az_copy(k, lax.rem(z - k + NZ, NZ)).wait_recv()
            self.ac_copy(core, x).start()
            for k in near_first(NX):
                self.ax_copy(k, x).start()

        def x_arrive(self, i):
            h = lax.rem(x + i, NX)
            self.ax_copy(NX - i, h).wait_recv()
            self.ac_copy(core, h).start()

        def partner_arrive(self, i):
            self.ac_copy(other, lax.rem(x + i, NX)).wait_recv()

        def sent(self):
            for h in range(KVH):
                self.core_copy(h).wait_send()
                self.ac_copy(core, h).wait_send()
            for k in range(1, NX):
                self.x_copy(k).wait_send()
                self.ax_copy(k, x).wait_send()
            for k in range(1, NZ):
                self.z_copy(k).wait_send()
                self.az_copy(k, z).wait_send()

    fwd = Sums(FWD, own1, csend1, crecv1, xsend1, xrecv1, xown1, zsend1, zrecv1, kv1)
    bwd = Sums(BWD, own2, csend2, crecv2, xsend2, xrecv2, xown2, zsend2, zrecv2, kv2)

    def w_loop(n, carry):
        near = lax.div(n + 1, 2)
        j = jnp.where(lax.rem(n, 2) == 1, near, lax.rem(NY - near, NY))

        @pl.when(n < NY)
        def _():
            b = lax.rem(t + j, NY)

            @pl.when(j != 0)
            def _():
                k = NY - j
                link(w_ref, w_all.at[b], WG + k, y_dev(k)).wait_recv()

            part = jnp.dot(vision_ref[0], w_all[b], preferred_element_type=F32)
            h = lax.rem(b, KVH)
            kind = lax.div(b, KVH)

            @pl.when(kind == core)
            def _():
                fwd.own[h] = part

            @pl.when(kind != core)
            def _():
                fwd.csend[h] = part.astype(BF16)
                fwd.core_copy(h).start()

        @pl.when(n >= NY - 2)
        def _():
            j = jnp.where(n < NY, n - (NY - 4), NY + 1 - n)
            fwd.x_step(lax.rem(t + j, KVH))

        return carry

    lax.fori_loop(0, NY + 2, w_loop, 0)
    fwd.z_stage()

    q_in.wait()
    do_in.wait()

    def turn(n):
        return jnp.where(n < 2, 1 + 2 * n, 6 - 2 * n)

    def out_copy(i):
        h = lax.rem(x + i, NX)
        span = pl.ds(pl.multiple_of(h * GROUP * HD, GROUP * HD), GROUP * HD)
        return pltpu.make_async_copy(dq_ref.at[:, span], dq_hbm.at[:, span], lsem.at[2 + i])

    def attend(n, carry):
        i = turn(n)
        h = lax.rem(x + i, NX)
        base = h * GROUP * HD

        def columns(j):
            return pl.ds(pl.multiple_of(base + j * HD, HD), HD)

        fwd.partner_arrive(i)
        kt_ref[...] = kv1[h].T

        def some_heads(m, inner):
            @pl.when((m == 1) & (n == 0))
            def _():
                fwd.x_arrive(2)

            @pl.when((m == 1) & (n > 0))
            def _():
                bwd.x_step(lax.rem(x + turn(n - 1), NX))

            dims = (((1,), (1,)), ((), ()))
            for r in range(GROUP // 2):
                j = m * (GROUP // 2) + r
                place = pl.ds(pl.multiple_of(j * HD, HD), HD)
                q_j = q_ref[:, columns(j)]
                do_j = do_ref[:, columns(j)]
                s = lax.dot_general(kv1[h], q_j, dims, preferred_element_type=F32)
                g = lax.dot_general(kv1[KVH + h], do_j, dims, preferred_element_type=F32)
                s = s * (SCALE * LOG2E) + bias_ref[...]
                e = jnp.exp2(s - jnp.max(s, axis=0, keepdims=True))
                probs = e * (1.0 / jnp.sum(e, axis=0, keepdims=True))
                delta = jnp.sum(probs * g, axis=0, keepdims=True)
                p_ref[:, place] = probs.astype(BF16)
                sg_ref[:, place] = (probs * (g - delta)).astype(BF16)
            return inner

        lax.fori_loop(0, 2, some_heads, 0)
        q_rows = jnp.concatenate([q_ref[:, columns(j)] for j in range(GROUP)], axis=0)
        do_rows = jnp.concatenate([do_ref[:, columns(j)] for j in range(GROUP)], axis=0)
        grads[0] = jnp.dot(sg_ref[...], q_rows, preferred_element_type=F32) * SCALE
        grads[1] = jnp.dot(p_ref[...], do_rows, preferred_element_type=F32)
        bwd.csend[h] = grads[other].astype(BF16)
        bwd.core_copy(h).start()
        bwd.own[h] = grads[core]
        dq_t = jnp.dot(kt_ref[...], sg_ref[...], preferred_element_type=F32) * SCALE
        for j in range(GROUP):
            dq_ref[:, columns(j)] = dq_t[:, j * HD : (j + 1) * HD].T.astype(BF16)
        out_copy(i).start()
        return carry

    fwd.x_arrive(1)
    fwd.x_arrive(3)
    lax.fori_loop(0, KVH, attend, 0)
    bwd.x_step(x)
    bwd.z_stage()

    def y_copy(k):
        return link(ysend.at[k], yrecv.at[k], YS + k, y_dev(k))

    images = xown1
    images[...] = jnp.zeros((TOK, HD), F32)

    def y_loop(n, carry):
        m = lax.rem(n, KVH)
        i = jnp.where(m < 2, m, 5 - m)
        kind = jnp.where(n < KVH, core, other)
        b = kind * KVH + lax.rem(x + i, NX)

        @pl.when((n > 0) & (n < KVH))
        def _():
            bwd.x_arrive(i)

        @pl.when(n >= KVH)
        def _():
            bwd.partner_arrive(i)

        part = jnp.dot(vt_ref[...], kv2[b], preferred_element_type=F32)
        k = lax.rem(b - t + NY, NY)

        @pl.when(k == 0)
        def _():
            yown[...] = part

        @pl.when(k != 0)
        def _():
            ysend[k] = part.astype(BF16)
            y_copy(k).start()

        images[...] += lax.dot_general(
            kv2[b], w_all[b], (((1,), (1,)), ((), ())), preferred_element_type=F32
        )
        return carry

    lax.fori_loop(0, 2 * KVH, y_loop, 0)
    vg_ref[0] = images[...].astype(BF16)

    grad = yown[...]
    for k in near_first(NY):
        y_copy(k).wait_recv()
        grad = grad + yrecv[k].astype(F32)
    wg_ref[...] = grad

    for i in range(KVH):
        out_copy(i).wait()
    fwd.sent()
    bwd.sent()
    for k in range(1, NY):
        w_copy(k).wait_send()
        y_copy(k).wait_send()


def local(queries, out_grad, vision, w_kv, links, img_count):
    rows, width = queries.shape
    anywhere = pl.BlockSpec(memory_space=pl.ANY)
    vmem = pl.BlockSpec(memory_space=pltpu.VMEM)
    smem = pl.BlockSpec(memory_space=pltpu.SMEM)
    sums = [
        pltpu.VMEM((KVH, TOK, HD), F32),
        pltpu.VMEM((KVH, TOK, HD), BF16),
        pltpu.VMEM((KVH, TOK, HD), BF16),
        pltpu.VMEM((NX, TOK, HD), BF16),
        pltpu.VMEM((NX, TOK, HD), BF16),
        pltpu.VMEM((TOK, HD), F32),
        pltpu.VMEM((TOK, HD), BF16),
        pltpu.VMEM((NZ, PIECE, HD), BF16),
        pltpu.VMEM((2 * KVH, TOK, HD), BF16),
    ]
    return pl.pallas_call(
        body,
        out_shape=(
            jax.ShapeDtypeStruct(queries.shape, BF16),
            jax.ShapeDtypeStruct(vision.shape, BF16),
            jax.ShapeDtypeStruct(w_kv.shape, F32),
        ),
        in_specs=[anywhere, anywhere, vmem, vmem, vmem, smem],
        out_specs=(anywhere, vmem, vmem),
        scratch_shapes=[
            pltpu.VMEM((rows, width), BF16),
            pltpu.VMEM((rows, width), BF16),
            pltpu.VMEM((rows, width), BF16),
            pltpu.VMEM((TOK, HD), F32),
            pltpu.VMEM((HD, TOK), BF16),
            pltpu.VMEM((HD, TOK), BF16),
            pltpu.VMEM((NY, HD, HD), BF16),
            pltpu.VMEM((TOK, GROUP * HD), BF16),
            pltpu.VMEM((TOK, GROUP * HD), BF16),
            pltpu.VMEM((2, TOK, HD), F32),
            *sums,
            *sums,
            pltpu.VMEM((NY, HD, HD), BF16),
            pltpu.VMEM((NY, HD, HD), BF16),
            pltpu.VMEM((HD, HD), F32),
            pltpu.SemaphoreType.DMA((SEMS,)),
            pltpu.SemaphoreType.DMA((SEMS,)),
            pltpu.SemaphoreType.DMA((6,)),
        ],
        compiler_params=pltpu.CompilerParams(
            collective_id=0, has_side_effects=True, vmem_limit_bytes=40 * 1024 * 1024
        ),
    )(queries, out_grad, vision, w_kv, jnp.swapaxes(links, 1, 2), img_count)


def solution(mesh):
    in_specs = (
        P(("txt", "vis"), None),
        P(("txt", "vis"), None),
        P("txt", None, "vis"),
        P("vis", "txt"),
        P("txt", None, None),
        P("txt"),
    )
    out_specs = (P(("txt", "vis"), None), P("txt", None, "vis"), P("vis", "txt"))
    return jax.shard_map(local, mesh=mesh, in_specs=in_specs, out_specs=out_specs, check_vma=False)
```

```python
import jax
import jax.numpy as jnp
from jax import lax
from jax.experimental import pallas as pl
from jax.experimental.pallas import tpu as pltpu
from jax.sharding import PartitionSpec as P

HD = 128
QH = 32
KVH = 4
GROUP = QH // KVH
IMG_DOC = 16
IMG_LEN = 24
TOK = IMG_DOC * IMG_LEN
NZ, NX, NY = 8, 4, 8
PIECE = TOK // NZ
SCALE = HD ** (-0.5)
LOG2E = 1.4426950408889634
MESH = pl.DeviceIdType.MESH
F32, BF16 = jnp.float32, jnp.bfloat16

CORE, XS, ZS, AZ, AX, AC = 0, 4, 8, 16, 24, 28
FWD, BWD, WG, YS = 0, 32, 64, 74
SEMS = 82


def near_first(n):
    return sorted(range(1, n), key=lambda k: min(k, n - k))


def far_first(n):
    return near_first(n)[::-1]


def body(
    q_hbm, do_hbm, vision_hbm, w_hbm, links_hbm, count_hbm,
    dq_hbm, vg_ref, wg_ref,
    q_ref, do_ref, dq_ref, vision_ref, links_ref, count_ref, bias_ref, vt_ref, w_all,
    p_ref, sg_ref, grads, images,
    own1, csend1, crecv1, xsend1, xrecv1, xown1, zsend1, zrecv1, kv1,
    csend2, crecv2, xsend2, xrecv2, xown2, zsend2, zrecv2, kv2,
    ysend, yrecv, yown,
    ssem, rsem, lsem,
):
    v = lax.axis_index("vis")
    t = lax.axis_index("txt")
    core = lax.rem(v, 2)
    x = lax.rem(lax.div(v, 2), NX)
    z = lax.div(v, 2 * NX)
    other = 1 - core
    mine = core * KVH + x

    def vis_at(zz, xx, cc):
        return (zz * NX + xx) * 2 + cc

    partner = (vis_at(z, x, other), t)

    def x_dev(k):
        return (vis_at(z, lax.rem(x + k, NX), core), t)

    def z_dev(k):
        return (vis_at(lax.rem(z + k, NZ), x, core), t)

    def y_dev(k):
        return (v, lax.rem(t + k, NY))

    def piece(zz):
        return pl.ds(pl.multiple_of(zz * PIECE, PIECE), PIECE)

    def link(src, dst, sem, dev):
        return pltpu.make_async_remote_copy(
            src_ref=src, dst_ref=dst, send_sem=ssem.at[sem], recv_sem=rsem.at[sem],
            device_id=dev, device_id_type=MESH,
        )

    fetches = [
        pltpu.make_async_copy(src, dst, lsem.at[n])
        for n, (src, dst) in enumerate([
            (w_hbm, w_all.at[t]), (vision_hbm, vision_ref), (links_hbm, links_ref),
            (count_hbm, count_ref), (q_hbm, q_ref), (do_hbm, do_ref),
        ])
    ]
    for fetch in fetches:
        fetch.start()

    barrier = pltpu.get_barrier_semaphore()
    partners = (
        [partner]
        + [x_dev(k) for k in range(1, NX)]
        + [z_dev(k) for k in range(1, NZ)]
        + [y_dev(k) for k in range(1, NY)]
    )
    for dev in partners:
        pl.semaphore_signal(barrier, inc=1, device_id=dev, device_id_type=MESH)
    pl.semaphore_wait(barrier, len(partners))

    def w_copy(k):
        return link(w_hbm, w_all.at[t], WG + NY - k, y_dev(k))

    def w_third(j):
        b = lax.rem(t + j, NY)
        up = j == 2
        return link(w_all.at[b], w_all.at[b], WG + (3 if up else 5), y_dev(NY - 1 if up else 1))

    def w_fourth(j):
        b = lax.rem(t + j, NY)
        up = j == 2
        half = w_all.at[b, pl.ds(0 if up else HD // 2, HD // 2), :]
        return link(half, half, WG + (4 if up else 8), y_dev(NY - 2 if up else 2))

    near_w = (1, NY - 1, 2, NY - 2)
    for k in near_w:
        w_copy(k).start()
    for fetch in fetches[:4]:
        fetch.wait()

    block = lax.broadcasted_iota(jnp.int32, links_ref.shape[1:], 1)
    slot = lax.broadcasted_iota(jnp.int32, (IMG_DOC, 1), 0)
    linked = jnp.sum(jnp.where(block == v, links_ref[0], 0), axis=1, keepdims=True)
    bias = jnp.where((linked == 1) & (slot < count_ref[0]), 0.0, -1e30)
    for s in range(IMG_DOC):
        bias_ref[s * IMG_LEN : (s + 1) * IMG_LEN, :] = jnp.broadcast_to(
            bias[s : s + 1, :], (IMG_LEN, HD)
        )
    vt_ref[...] = vision_ref[0].T

    class Sums:
        def __init__(self, base, own_at, csend, crecv, xsend, xrecv, xown, zsend, zrecv, kv):
            self.base, self.own_at, self.csend, self.crecv = base, own_at, csend, crecv
            self.xsend, self.xrecv, self.xown = xsend, xrecv, xown
            self.zsend, self.zrecv, self.kv = zsend, zrecv, kv

        def core_copy(self, h):
            return link(self.csend.at[h], self.crecv.at[h], self.base + CORE + h, partner)

        def x_copy(self, k):
            return link(self.xsend.at[k], self.xrecv.at[k], self.base + XS + k, x_dev(k))

        def z_copy(self, k):
            rows = piece(lax.rem(z + k, NZ))
            return link(self.zsend.at[rows, :], self.zrecv.at[k], self.base + ZS + k, z_dev(k))

        def az_copy(self, k, zz):
            ref = self.kv.at[mine, piece(zz), :]
            return link(ref, ref, self.base + AZ + k, z_dev(k))

        def ax_copy(self, k, h):
            ref = self.kv.at[core * KVH + h]
            return link(ref, ref, self.base + AX + k, x_dev(k))

        def ac_copy(self, kind, h):
            ref = self.kv.at[kind * KVH + h]
            return link(ref, ref, self.base + AC + h, partner)

        def x_step(self, h):
            self.core_copy(h).wait_recv()
            total = self.own_at(h) + self.crecv[h].astype(F32)
            k = lax.rem(h - x + NX, NX)

            @pl.when(k == 0)
            def _():
                self.xown[...] = total

            @pl.when(k != 0)
            def _():
                self.xsend[k] = total.astype(BF16)
                self.x_copy(k).start()

        def z_stage(self, first=lambda: None, second=lambda: None):
            total = self.xown[...]
            for k in near_first(NX):
                self.x_copy(k).wait_recv()
                total = total + self.xrecv[k].astype(F32)
            self.xown[...] = total
            self.zsend[...] = total.astype(BF16)
            for k in far_first(NZ):
                self.z_copy(k).start()
            first()
            part = self.xown[piece(z), :]
            for k in near_first(NZ):
                self.z_copy(k).wait_recv()
                part = part + self.zrecv[k].astype(F32)
            self.kv[mine, piece(z), :] = part.astype(BF16)
            for k in far_first(NZ):
                self.az_copy(k, z).start()
            second()
            for k in near_first(NZ):
                self.az_copy(k, lax.rem(z - k + NZ, NZ)).wait_recv()
            self.ac_copy(core, x).start()
            for k in near_first(NX):
                self.ax_copy(k, x).start()

        def x_arrive(self, i):
            h = lax.rem(x + i, NX)
            self.ax_copy(NX - i, h).wait_recv()
            self.ac_copy(core, h).start()

        def partner_arrive(self, i):
            self.ac_copy(other, lax.rem(x + i, NX)).wait_recv()

        def sent(self):
            for h in range(KVH):
                self.core_copy(h).wait_send()
                self.ac_copy(core, h).wait_send()
            for k in range(1, NX):
                self.x_copy(k).wait_send()
                self.ax_copy(k, x).wait_send()
            for k in range(1, NZ):
                self.z_copy(k).wait_send()
                self.az_copy(k, z).wait_send()

    fwd = Sums(FWD, lambda h: own1[h], csend1, crecv1, xsend1, xrecv1, xown1, zsend1, zrecv1, kv1)
    bwd = Sums(BWD, lambda h: grads[h, core], csend2, crecv2, xsend2, xrecv2, xown2, zsend2, zrecv2, kv2)

    def near(n):
        far = lax.div(n + 1, 2)
        return jnp.where(lax.rem(n, 2) == 1, far, lax.rem(NY - far, NY))

    def w_loop(n, carry):
        @pl.when(n < NY)
        def _():
            j = near(n)
            b = lax.rem(t + j, NY)

            @pl.when((j != 0) & (j != 4))
            def _():
                link(w_hbm, w_all.at[b], WG + j, y_dev(1)).wait_recv()

            for hop in (2, 6):
                @pl.when(j == hop)
                def _():
                    w_third(hop).start()
                    w_fourth(hop).start()

            @pl.when(j == 4)
            def _():
                for place, low in ((4, 0), (8, HD // 2)):
                    half = w_all.at[b, pl.ds(low, HD // 2), :]
                    link(half, half, WG + place, y_dev(2)).wait_recv()

            part = jnp.dot(vision_ref[0], w_all[b], preferred_element_type=F32)
            h = lax.rem(b, KVH)
            kind = lax.div(b, KVH)

            @pl.when(kind == core)
            def _():
                own1[h] = part

            @pl.when(kind != core)
            def _():
                fwd.csend[h] = part.astype(BF16)
                fwd.core_copy(h).start()

        past = lax.rem(t + near(jnp.maximum(n - 2, 0)), NY)

        @pl.when((n >= 2) & (lax.div(past, KVH) == core))
        def _():
            fwd.x_step(lax.rem(past, KVH))

        return carry

    lax.fori_loop(0, NY + 2, w_loop, 0)
    fwd.z_stage()

    for fetch in fetches[4:]:
        fetch.wait()

    HALF = GROUP // 2

    def attend(u, carry):
        mine_now = (u == 0) | (u == 2 * KVH - 1)
        i = jnp.where(mine_now, 0, jnp.where(u >= 5, 2, jnp.where(u >= 3, 3, 1)))
        half = jnp.where(mine_now, lax.div(u, 2 * KVH - 1), lax.rem(u + 1, 2))
        h = lax.rem(x + i, NX)
        base = h * GROUP * HD + half * HALF * HD

        def columns(j):
            return pl.ds(pl.multiple_of(base + j * HD, HD), HD)

        @pl.when(u == 1)
        def _():
            fwd.x_arrive(1)

        @pl.when(half == 0)
        def _():
            fwd.partner_arrive(i)

        q = [q_ref[:, columns(j)] for j in range(HALF)]
        do = [do_ref[:, columns(j)] for j in range(HALF)]
        dims = (((1,), (1,)), ((), ()))
        bias = jnp.concatenate([bias_ref[...]] * 2, axis=1)
        for j in range(0, HALF, 2):
            two_q = jnp.concatenate(q[j : j + 2], axis=0)
            two_do = jnp.concatenate(do[j : j + 2], axis=0)
            s = lax.dot_general(kv1[h], two_q, dims, preferred_element_type=F32)
            g = lax.dot_general(kv1[KVH + h], two_do, dims, preferred_element_type=F32)
            s = s * (SCALE * LOG2E) + bias
            e = jnp.exp2(s - jnp.max(s, axis=0, keepdims=True))
            probs = e * (1.0 / jnp.sum(e, axis=0, keepdims=True))
            delta = jnp.sum(probs * g, axis=0, keepdims=True)
            p_ref[:, j * HD : (j + 2) * HD] = probs.astype(BF16)
            place = pl.ds(pl.multiple_of((half * HALF + j) * HD, HD), 2 * HD)
            sg_ref[h, :, place] = (probs * (g - delta)).astype(BF16)

        @pl.when(u == 1)
        def _():
            fwd.x_arrive(3)

        @pl.when(u == 3)
        def _():
            fwd.x_arrive(2)

        for when, done in ((4, 1), (6, 3), (7, 2)):
            @pl.when(u == when)
            def _():
                bwd.x_step(lax.rem(x + done, NX))

        place = pl.ds(pl.multiple_of(half * HALF * HD, HALF * HD), HALF * HD)
        key_part = jnp.dot(
            sg_ref[h, :, place], jnp.concatenate(q, axis=0), preferred_element_type=F32
        ) * SCALE
        value_part = jnp.dot(
            p_ref[...], jnp.concatenate(do, axis=0), preferred_element_type=F32
        )

        @pl.when(half == 0)
        def _():
            grads[h, 0] = key_part
            grads[h, 1] = value_part

        @pl.when(half == 1)
        def _():
            grads[h, 0] += key_part
            grads[h, 1] += value_part
            bwd.csend[h] = grads[h, other].astype(BF16)
            bwd.core_copy(h).start()

        return carry

    lax.fori_loop(0, 2 * KVH, attend, 0)

    def dq_copy(i):
        span = pl.ds(pl.multiple_of(lax.rem(x + i, NX) * GROUP * HD, GROUP * HD), GROUP * HD)
        return pltpu.make_async_copy(dq_ref.at[:, span], dq_hbm.at[:, span], lsem.at[6 + i])

    def query_grads(low, high):
        def one(i, carry):
            h = lax.rem(x + i, NX)
            dq = jnp.dot(kv1[h].T, sg_ref[h], preferred_element_type=F32) * SCALE
            for j in range(GROUP):
                place = pl.ds(pl.multiple_of((h * GROUP + j) * HD, HD), HD)
                dq_ref[:, place] = dq[:, j * HD : (j + 1) * HD].T.astype(BF16)
            dq_copy(i).start()
            return carry

        lax.fori_loop(low, high, one, 0)

    query_grads(0, 1)
    bwd.x_step(x)
    bwd.z_stage(lambda: query_grads(1, 3), lambda: query_grads(3, KVH))

    def y_copy(k):
        return link(ysend.at[k], yrecv.at[k], YS + k, y_dev(k))

    images[...] = jnp.zeros((TOK, HD), F32)

    def y_loop(n, carry):
        i = jnp.where(n < 2, 0, jnp.where(n >= 6, 2, 1 + 2 * lax.rem(n, 2)))
        here = (n == 0) | (n == 2) | (n == 3) | (n == 6)
        kind = jnp.where(here, core, other)
        b = kind * KVH + lax.rem(x + i, NX)

        @pl.when(here & (n > 0))
        def _():
            bwd.x_arrive(i)

        @pl.when(jnp.logical_not(here))
        def _():
            bwd.partner_arrive(i)

        part = jnp.dot(vt_ref[...], kv2[b], preferred_element_type=F32)
        k = lax.rem(b - t + NY, NY)

        @pl.when(k == 0)
        def _():
            yown[...] = part

        @pl.when(k != 0)
        def _():
            ysend[k] = part.astype(BF16)
            y_copy(k).start()

        images[...] += lax.dot_general(
            kv2[b], w_all[b], (((1,), (1,)), ((), ())), preferred_element_type=F32
        )
        return carry

    lax.fori_loop(0, 2 * KVH, y_loop, 0)
    vg_ref[0] = images[...].astype(BF16)

    grad = yown[...]
    for k in near_first(NY):
        y_copy(k).wait_recv()
        grad = grad + yrecv[k].astype(F32)
    wg_ref[...] = grad

    for i in range(KVH):
        dq_copy(i).wait()
    fwd.sent()
    bwd.sent()
    for k in near_w:
        w_copy(k).wait_send()
    for hop in (2, 6):
        w_third(hop).wait_send()
        w_fourth(hop).wait_send()
    for k in range(1, NY):
        y_copy(k).wait_send()


def write(*refs):
    sources, targets, sem = refs[:3], refs[3:6], refs[6]
    copies = [
        pltpu.make_async_copy(src, dst, sem.at[n])
        for n, (src, dst) in enumerate(zip(sources, targets))
    ]
    for copy in copies:
        copy.start()
    for copy in copies:
        copy.wait()


def local(queries, out_grad, vision, w_kv, links, img_count):
    rows, width = queries.shape
    anywhere = pl.BlockSpec(memory_space=pl.ANY)
    hbm = pl.BlockSpec(memory_space=pltpu.HBM)
    vmem = pl.BlockSpec(memory_space=pltpu.VMEM)
    sums = [
        pltpu.VMEM((KVH, TOK, HD), BF16),
        pltpu.VMEM((KVH, TOK, HD), BF16),
        pltpu.VMEM((NX, TOK, HD), BF16),
        pltpu.VMEM((NX, TOK, HD), BF16),
        pltpu.VMEM((TOK, HD), F32),
        pltpu.VMEM((TOK, HD), BF16),
        pltpu.VMEM((NZ, PIECE, HD), BF16),
        pltpu.VMEM((2 * KVH, TOK, HD), BF16),
    ]
    link_slots = jnp.swapaxes(links, 1, 2)
    out_shape = (
        jax.ShapeDtypeStruct(queries.shape, BF16),
        jax.ShapeDtypeStruct(vision.shape, BF16),
        jax.ShapeDtypeStruct(w_kv.shape, F32),
    )
    results = pl.pallas_call(
        body,
        out_shape=out_shape,
        in_specs=[hbm] * 6,
        out_specs=(hbm, vmem, vmem),
        scratch_shapes=[
            pltpu.VMEM((rows, width), BF16),
            pltpu.VMEM((rows, width), BF16),
            pltpu.VMEM((rows, width), BF16),
            pltpu.VMEM(vision.shape, BF16),
            pltpu.VMEM(link_slots.shape, jnp.int32),
            pltpu.SMEM(img_count.shape, jnp.int32),
            pltpu.VMEM((TOK, HD), F32),
            pltpu.VMEM((HD, TOK), BF16),
            pltpu.VMEM((NY, HD, HD), BF16),
            pltpu.VMEM((TOK, GROUP // 2 * HD), BF16),
            pltpu.VMEM((KVH, TOK, GROUP * HD), BF16),
            pltpu.VMEM((KVH, 2, TOK, HD), F32),
            pltpu.VMEM((TOK, HD), F32),
            pltpu.VMEM((KVH, TOK, HD), F32),
            *sums,
            *sums,
            pltpu.VMEM((NY, HD, HD), BF16),
            pltpu.VMEM((NY, HD, HD), BF16),
            pltpu.VMEM((HD, HD), F32),
            pltpu.SemaphoreType.DMA((SEMS,)),
            pltpu.SemaphoreType.DMA((SEMS,)),
            pltpu.SemaphoreType.DMA((6 + KVH,)),
        ],
        compiler_params=pltpu.CompilerParams(
            collective_id=0, has_side_effects=True, vmem_limit_bytes=60 * 1024 * 1024
        ),
    )(queries, out_grad, vision, w_kv, link_slots, img_count)
    return pl.pallas_call(
        write,
        out_shape=out_shape,
        in_specs=[anywhere] * 3,
        out_specs=(hbm,) * 3,
        scratch_shapes=[pltpu.SemaphoreType.DMA((3,))],
        compiler_params=pltpu.CompilerParams(vmem_limit_bytes=60 * 1024 * 1024),
    )(*results)


def solution(mesh):
    in_specs = (
        P(("txt", "vis"), None),
        P(("txt", "vis"), None),
        P("txt", None, "vis"),
        P("vis", "txt"),
        P("txt", None, None),
        P("txt"),
    )
    out_specs = (P(("txt", "vis"), None), P("txt", None, "vis"), P("vis", "txt"))
    return jax.shard_map(local, mesh=mesh, in_specs=in_specs, out_specs=out_specs, check_vma=False)
```

```python
import jax
import jax.numpy as jnp
from jax import lax
from jax.experimental import pallas as pl
from jax.experimental.pallas import tpu as pltpu
from jax.sharding import PartitionSpec as P

HD = 128
QH = 32
KVH = 4
GROUP = QH // KVH
IMG_DOC = 16
IMG_LEN = 24
TOK = IMG_DOC * IMG_LEN
NZ, NX, NY = 8, 4, 8
PIECE = TOK // NZ
SCALE = HD ** (-0.5)
LOG2E = 1.4426950408889634
MESH = pl.DeviceIdType.MESH
F32, BF16 = jnp.float32, jnp.bfloat16

CORE, XS, ZS, AZ, AX, AC = 0, 4, 8, 16, 24, 29
FWD, BWD, WG, YS = 0, 33, 66, 76
SEMS = 84


def near_first(n):
    return sorted(range(1, n), key=lambda k: min(k, n - k))


def far_first(n):
    return near_first(n)[::-1]


def body(
    q_hbm, do_hbm, vision_hbm, w_hbm, links_hbm, count_hbm,
    dq_hbm, vg_ref, wg_ref,
    q_ref, do_ref, dq_ref, vision_ref, links_ref, count_ref, bias_ref, vt_ref, w_all,
    sg_ref, grads, images,
    own1, csend1, crecv1, xsend1, xrecv1, xown1, zsend1, zrecv1, kv1,
    csend2, crecv2, xsend2, xrecv2, xown2, zsend2, zrecv2, kv2,
    ysend, yrecv, yown,
    ssem, rsem, lsem,
):
    v = lax.axis_index("vis")
    t = lax.axis_index("txt")
    core = lax.rem(v, 2)
    x = lax.rem(lax.div(v, 2), NX)
    z = lax.div(v, 2 * NX)
    other = 1 - core
    mine = core * KVH + x

    def vis_at(zz, xx, cc):
        return (zz * NX + xx) * 2 + cc

    partner = (vis_at(z, x, other), t)

    def x_dev(k):
        return (vis_at(z, lax.rem(x + k, NX), core), t)

    def z_dev(k):
        return (vis_at(lax.rem(z + k, NZ), x, core), t)

    def y_dev(k):
        return (v, lax.rem(t + k, NY))

    def piece(zz):
        return pl.ds(pl.multiple_of(zz * PIECE, PIECE), PIECE)

    def link(src, dst, sem, dev):
        return pltpu.make_async_remote_copy(
            src_ref=src, dst_ref=dst, send_sem=ssem.at[sem], recv_sem=rsem.at[sem],
            device_id=dev, device_id_type=MESH,
        )

    fetches = [
        pltpu.make_async_copy(src, dst, lsem.at[n])
        for n, (src, dst) in enumerate([
            (w_hbm, w_all.at[t]), (vision_hbm, vision_ref), (links_hbm, links_ref),
            (count_hbm, count_ref), (q_hbm, q_ref), (do_hbm, do_ref),
        ])
    ]
    for fetch in fetches:
        fetch.start()

    barrier = pltpu.get_barrier_semaphore()
    partners = (
        [partner]
        + [x_dev(k) for k in range(1, NX)]
        + [z_dev(k) for k in range(1, NZ)]
        + [y_dev(k) for k in range(1, NY)]
    )
    for dev in partners:
        pl.semaphore_signal(barrier, inc=1, device_id=dev, device_id_type=MESH)
    pl.semaphore_wait(barrier, len(partners))

    def w_copy(k):
        return link(w_hbm, w_all.at[t], WG + NY - k, y_dev(k))

    def w_third(j):
        b = lax.rem(t + j, NY)
        up = j == 2
        return link(w_all.at[b], w_all.at[b], WG + (3 if up else 5), y_dev(NY - 1 if up else 1))

    def w_fourth(j):
        b = lax.rem(t + j, NY)
        up = j == 2
        half = w_all.at[b, pl.ds(0 if up else HD // 2, HD // 2), :]
        return link(half, half, WG + (4 if up else 8), y_dev(NY - 2 if up else 2))

    near_w = (1, NY - 1, 2, NY - 2)
    for k in near_w:
        w_copy(k).start()
    for fetch in fetches[:4]:
        fetch.wait()

    block = lax.broadcasted_iota(jnp.int32, links_ref.shape[1:], 1)
    slot = lax.broadcasted_iota(jnp.int32, (IMG_DOC, 1), 0)
    linked = jnp.sum(jnp.where(block == v, links_ref[0], 0), axis=1, keepdims=True)
    bias = jnp.where((linked == 1) & (slot < count_ref[...]), 0.0, -1e30)
    for s in range(IMG_DOC):
        bias_ref[s * IMG_LEN : (s + 1) * IMG_LEN, :] = jnp.broadcast_to(
            bias[s : s + 1, :], (IMG_LEN, HD)
        )
    vt_ref[...] = vision_ref[0].T

    class Sums:
        def __init__(self, base, own_at, csend, crecv, xsend, xrecv, xown, zsend, zrecv, kv):
            self.base, self.own_at, self.csend, self.crecv = base, own_at, csend, crecv
            self.xsend, self.xrecv, self.xown = xsend, xrecv, xown
            self.zsend, self.zrecv, self.kv = zsend, zrecv, kv

        def core_copy(self, h):
            return link(self.csend.at[h], self.crecv.at[h], self.base + CORE + h, partner)

        def x_copy(self, k):
            return link(self.xsend.at[k], self.xrecv.at[k], self.base + XS + k, x_dev(k))

        def z_copy(self, k):
            rows = piece(lax.rem(z + k, NZ))
            return link(self.zsend.at[rows, :], self.zrecv.at[k], self.base + ZS + k, z_dev(k))

        def az_copy(self, k, zz):
            ref = self.kv.at[mine, piece(zz), :]
            return link(ref, ref, self.base + AZ + k, z_dev(k))

        def ax_copy(self, k, h):
            ref = self.kv.at[core * KVH + h]
            return link(ref, ref, self.base + AX + k, x_dev(k))

        def across(self, i):
            h = lax.rem(x + i, NX)
            up = i == 1
            half = self.kv.at[core * KVH + h, pl.ds(0 if up else TOK // 2, TOK // 2), :]
            return link(half, half, self.base + AX + (2 if up else 4), x_dev(3 if up else 1))

        def ac_copy(self, kind, h):
            ref = self.kv.at[kind * KVH + h]
            return link(ref, ref, self.base + AC + h, partner)

        def x_step(self, h):
            self.core_copy(h).wait_recv()
            total = self.own_at(h) + self.crecv[h].astype(F32)
            k = lax.rem(h - x + NX, NX)

            @pl.when(k == 0)
            def _():
                self.xown[...] = total

            @pl.when(k != 0)
            def _():
                self.xsend[k] = total.astype(BF16)
                self.x_copy(k).start()

        def z_stage(self, first=lambda: None, second=lambda: None):
            total = self.xown[...]
            for k in near_first(NX):
                self.x_copy(k).wait_recv()
                total = total + self.xrecv[k].astype(F32)
            self.xown[...] = total
            self.zsend[...] = total.astype(BF16)
            for k in far_first(NZ):
                self.z_copy(k).start()
            first()
            part = self.xown[piece(z), :]
            for k in near_first(NZ):
                self.z_copy(k).wait_recv()
                part = part + self.zrecv[k].astype(F32)
            self.kv[mine, piece(z), :] = part.astype(BF16)
            for k in far_first(NZ):
                self.az_copy(k, z).start()
            second()
            for k in near_first(NZ):
                self.az_copy(k, lax.rem(z - k + NZ, NZ)).wait_recv()
            self.ac_copy(core, x).start()
            for k in (1, 3):
                self.ax_copy(k, x).start()

        def x_arrive(self, i):
            h = lax.rem(x + i, NX)
            if i == 2:
                for place, low in ((2, 0), (4, TOK // 2)):
                    half = self.kv.at[core * KVH + h, pl.ds(low, TOK // 2), :]
                    link(half, half, self.base + AX + place, x_dev(1)).wait_recv()
            else:
                self.ax_copy(NX - i, h).wait_recv()
                self.across(i).start()
            self.ac_copy(core, h).start()

        def partner_arrive(self, i):
            self.ac_copy(other, lax.rem(x + i, NX)).wait_recv()

        def sent(self):
            for h in range(KVH):
                self.core_copy(h).wait_send()
                self.ac_copy(core, h).wait_send()
            for k in range(1, NX):
                self.x_copy(k).wait_send()
            for k in (1, 3):
                self.ax_copy(k, x).wait_send()
                self.across(k).wait_send()
            for k in range(1, NZ):
                self.z_copy(k).wait_send()
                self.az_copy(k, z).wait_send()

    fwd = Sums(FWD, lambda h: own1[h], csend1, crecv1, xsend1, xrecv1, xown1, zsend1, zrecv1, kv1)
    bwd = Sums(BWD, lambda h: grads[h, core], csend2, crecv2, xsend2, xrecv2, xown2, zsend2, zrecv2, kv2)

    def near(n):
        far = lax.div(n + 1, 2)
        return jnp.where(lax.rem(n, 2) == 1, far, lax.rem(NY - far, NY))

    def w_loop(n, carry):
        @pl.when(n < NY)
        def _():
            j = near(n)
            b = lax.rem(t + j, NY)

            @pl.when((j != 0) & (j != 4))
            def _():
                link(w_hbm, w_all.at[b], WG + j, y_dev(1)).wait_recv()

            for hop in (2, 6):
                @pl.when(j == hop)
                def _():
                    w_third(hop).start()
                    w_fourth(hop).start()

            @pl.when(j == 4)
            def _():
                for place, low in ((4, 0), (8, HD // 2)):
                    half = w_all.at[b, pl.ds(low, HD // 2), :]
                    link(half, half, WG + place, y_dev(2)).wait_recv()

            part = jnp.dot(vision_ref[0], w_all[b], preferred_element_type=F32)
            h = lax.rem(b, KVH)
            kind = lax.div(b, KVH)

            @pl.when(kind == core)
            def _():
                own1[h] = part

            @pl.when(kind != core)
            def _():
                fwd.csend[h] = part.astype(BF16)
                fwd.core_copy(h).start()

        past = lax.rem(t + near(jnp.maximum(n - 2, 0)), NY)

        @pl.when((n >= 2) & (lax.div(past, KVH) == core))
        def _():
            fwd.x_step(lax.rem(past, KVH))

        return carry

    lax.fori_loop(0, NY + 2, w_loop, 0)
    fwd.z_stage()

    for fetch in fetches[4:]:
        fetch.wait()

    HALF = GROUP // 2

    def attend(u, carry):
        mine_now = (u == 0) | (u == 2 * KVH - 1)
        i = jnp.where(mine_now, 0, lax.div(u + 1, 2))
        half = jnp.where(mine_now, lax.div(u, 2 * KVH - 1), lax.rem(u + 1, 2))
        h = lax.rem(x + i, NX)
        base = h * GROUP * HD + half * HALF * HD

        def columns(j):
            return pl.ds(pl.multiple_of(base + j * HD, HD), HD)

        @pl.when(u == 1)
        def _():
            fwd.x_arrive(1)
            fwd.x_arrive(3)

        @pl.when(u == 2)
        def _():
            fwd.x_arrive(2)

        @pl.when(half == 0)
        def _():
            fwd.partner_arrive(i)

        dims = (((1,), (1,)), ((), ()))
        bias = jnp.concatenate([bias_ref[...]] * 2, axis=1)
        key_part = value_part = None
        for j in range(0, HALF, 2):
            q = jnp.concatenate([q_ref[:, columns(j)], q_ref[:, columns(j + 1)]], axis=0)
            do = jnp.concatenate([do_ref[:, columns(j)], do_ref[:, columns(j + 1)]], axis=0)
            s = lax.dot_general(kv1[h], q, dims, preferred_element_type=F32)
            g = lax.dot_general(kv1[KVH + h], do, dims, preferred_element_type=F32)
            s = s * (SCALE * LOG2E) + bias
            e = jnp.exp2(s - jnp.max(s, axis=0, keepdims=True))
            norm = 1.0 / jnp.sum(e, axis=0, keepdims=True)
            delta = jnp.sum(e * g, axis=0, keepdims=True) * norm
            probs = e * norm
            score_grad = (probs * (g - delta)).astype(BF16)
            place = pl.ds(pl.multiple_of((half * HALF + j) * HD, HD), 2 * HD)
            sg_ref[h, :, place] = score_grad
            key_more = jnp.dot(score_grad, q, preferred_element_type=F32)
            value_more = jnp.dot(probs.astype(BF16), do, preferred_element_type=F32)
            key_part = key_more if j == 0 else key_part + key_more
            value_part = value_more if j == 0 else value_part + value_more
        key_part = key_part * SCALE

        for when, done in ((3, 1), (5, 2), (7, 3)):
            @pl.when(u == when)
            def _():
                bwd.x_step(lax.rem(x + done, NX))

        @pl.when(half == 0)
        def _():
            grads[h, 0] = key_part
            grads[h, 1] = value_part

        @pl.when(half == 1)
        def _():
            grads[h, 0] += key_part
            grads[h, 1] += value_part
            bwd.csend[h] = grads[h, other].astype(BF16)
            bwd.core_copy(h).start()

        return carry

    lax.fori_loop(0, 2 * KVH, attend, 0)

    def dq_copy(i):
        span = pl.ds(pl.multiple_of(lax.rem(x + i, NX) * GROUP * HD, GROUP * HD), GROUP * HD)
        return pltpu.make_async_copy(dq_ref.at[:, span], dq_hbm.at[:, span], lsem.at[6 + i])

    def query_grads(low, high):
        def one(i, carry):
            h = lax.rem(x + i, NX)
            dq = jnp.dot(kv1[h].T, sg_ref[h], preferred_element_type=F32) * SCALE
            for j in range(GROUP):
                place = pl.ds(pl.multiple_of((h * GROUP + j) * HD, HD), HD)
                dq_ref[:, place] = dq[:, j * HD : (j + 1) * HD].T.astype(BF16)
            dq_copy(i).start()
            return carry

        lax.fori_loop(low, high, one, 0)

    query_grads(0, 1)
    bwd.x_step(x)
    bwd.z_stage(lambda: query_grads(1, 3), lambda: query_grads(3, KVH))

    def y_copy(k):
        return link(ysend.at[k], yrecv.at[k], YS + k, y_dev(k))

    images[...] = jnp.zeros((TOK, HD), F32)

    def y_loop(n, carry):
        i = jnp.where(n < 2, 0, jnp.where(n >= 6, 2, 1 + 2 * lax.rem(n, 2)))
        here = (n == 0) | (n == 2) | (n == 3) | (n == 6)
        kind = jnp.where(here, core, other)
        b = kind * KVH + lax.rem(x + i, NX)

        for when, place in ((2, 1), (3, 3), (6, 2)):
            @pl.when(n == when)
            def _():
                bwd.x_arrive(place)

        @pl.when(jnp.logical_not(here))
        def _():
            bwd.partner_arrive(i)

        part = jnp.dot(vt_ref[...], kv2[b], preferred_element_type=F32)
        k = lax.rem(b - t + NY, NY)

        @pl.when(k == 0)
        def _():
            yown[...] = part

        @pl.when(k != 0)
        def _():
            ysend[k] = part.astype(BF16)
            y_copy(k).start()

        images[...] += lax.dot_general(
            kv2[b], w_all[b], (((1,), (1,)), ((), ())), preferred_element_type=F32
        )
        return carry

    lax.fori_loop(0, 2 * KVH, y_loop, 0)
    vg_ref[0] = images[...].astype(BF16)

    for i in range(KVH):
        dq_copy(i).wait()
    fwd.sent()
    bwd.sent()
    for k in near_w:
        w_copy(k).wait_send()
    for hop in (2, 6):
        w_third(hop).wait_send()
        w_fourth(hop).wait_send()

    grad = yown[...]
    for k in near_first(NY):
        y_copy(k).wait_recv()
        grad = grad + yrecv[k].astype(F32)
    wg_ref[...] = grad
    for k in range(1, NY):
        y_copy(k).wait_send()


def local(queries, out_grad, vision, w_kv, links, img_count):
    rows, width = queries.shape
    hbm = pl.BlockSpec(memory_space=pltpu.HBM)
    vmem = pl.BlockSpec(memory_space=pltpu.VMEM)
    sums = [
        pltpu.VMEM((KVH, TOK, HD), BF16),
        pltpu.VMEM((KVH, TOK, HD), BF16),
        pltpu.VMEM((NX, TOK, HD), BF16),
        pltpu.VMEM((NX, TOK, HD), BF16),
        pltpu.VMEM((TOK, HD), F32),
        pltpu.VMEM((TOK, HD), BF16),
        pltpu.VMEM((NZ, PIECE, HD), BF16),
        pltpu.VMEM((2 * KVH, TOK, HD), BF16),
    ]
    link_slots = jnp.swapaxes(links, 1, 2)
    out_shape = (
        jax.ShapeDtypeStruct(queries.shape, BF16),
        jax.ShapeDtypeStruct(vision.shape, BF16),
        jax.ShapeDtypeStruct(w_kv.shape, F32),
    )
    return pl.pallas_call(
        body,
        out_shape=out_shape,
        in_specs=[hbm] * 6,
        out_specs=(hbm, vmem, vmem),
        scratch_shapes=[
            pltpu.VMEM((rows, width), BF16),
            pltpu.VMEM((rows, width), BF16),
            pltpu.VMEM((rows, width), BF16),
            pltpu.VMEM(vision.shape, BF16),
            pltpu.VMEM(link_slots.shape, jnp.int32),
            pltpu.VMEM((1, 1), jnp.int32),
            pltpu.VMEM((TOK, HD), F32),
            pltpu.VMEM((HD, TOK), BF16),
            pltpu.VMEM((NY, HD, HD), BF16),
            pltpu.VMEM((KVH, TOK, GROUP * HD), BF16),
            pltpu.VMEM((KVH, 2, TOK, HD), F32),
            pltpu.VMEM((TOK, HD), F32),
            pltpu.VMEM((KVH, TOK, HD), F32),
            *sums,
            *sums,
            pltpu.VMEM((NY, HD, HD), BF16),
            pltpu.VMEM((NY, HD, HD), BF16),
            pltpu.VMEM((HD, HD), F32),
            pltpu.SemaphoreType.DMA((SEMS,)),
            pltpu.SemaphoreType.DMA((SEMS,)),
            pltpu.SemaphoreType.DMA((6 + KVH,)),
        ],
        compiler_params=pltpu.CompilerParams(
            collective_id=0, has_side_effects=True, vmem_limit_bytes=60 * 1024 * 1024
        ),
    )(queries, out_grad, vision, w_kv, link_slots, img_count.reshape(1, 1))


def solution(mesh):
    in_specs = (
        P(("txt", "vis"), None),
        P(("txt", "vis"), None),
        P("txt", None, "vis"),
        P("vis", "txt"),
        P("txt", None, None),
        P("txt"),
    )
    out_specs = (P(("txt", "vis"), None), P("txt", None, "vis"), P("vis", "txt"))
    return jax.shard_map(local, mesh=mesh, in_specs=in_specs, out_specs=out_specs, check_vma=False)
```

```python
import jax
import jax.numpy as jnp
from jax import lax
from jax.experimental import pallas as pl
from jax.experimental.pallas import tpu as pltpu
from jax.sharding import PartitionSpec as P

HD = 128
QH = 32
KVH = 4
GROUP = QH // KVH
IMG_DOC = 16
IMG_LEN = 24
TOK = IMG_DOC * IMG_LEN
NZ, NX, NY = 8, 4, 8
PIECE = TOK // NZ
SCALE = HD ** (-0.5)
LOG2E = 1.4426950408889634
MESH = pl.DeviceIdType.MESH
F32, BF16 = jnp.float32, jnp.bfloat16

CORE, XS, ZS, AZ, AX, AC = 0, 4, 8, 16, 24, 29
FWD, BWD, WG, YS, VS, VG = 0, 33, 66, 84, 92, 93
SEMS = 94


def near_first(n):
    return sorted(range(1, n), key=lambda k: min(k, n - k))


def far_first(n):
    return near_first(n)[::-1]


def body(
    q_hbm, do_hbm, vision_hbm, w_hbm, links_hbm, count_hbm,
    dq_ref, vg_ref, wg_ref,
    q_ref, do_ref, vision_ref, links_ref, count_ref, bias_ref, vt_ref, w_all, vg_send, vg_recv,
    sg_ref, grads, images,
    xsend1, xrecv1, xown1, zsend1, zrecv1, kv1,
    csend, crecv, xsend2, xrecv2, xown2, zsend2, zrecv2, kv2,
    ysend, yrecv, yown,
    ssem, rsem, lsem,
):
    v = lax.axis_index("vis")
    t = lax.axis_index("txt")
    core = lax.rem(v, 2)
    x = lax.rem(lax.div(v, 2), NX)
    z = lax.div(v, 2 * NX)
    other = 1 - core
    mine = core * KVH + x

    def vis_at(zz, xx, cc):
        return (zz * NX + xx) * 2 + cc

    partner = (vis_at(z, x, other), t)

    def x_dev(k):
        return (vis_at(z, lax.rem(x + k, NX), core), t)

    def z_dev(k):
        return (vis_at(lax.rem(z + k, NZ), x, core), t)

    def y_dev(k, cc=core):
        return (vis_at(z, x, cc), lax.rem(t + k, NY))

    def piece(zz):
        return pl.ds(pl.multiple_of(zz * PIECE, PIECE), PIECE)

    def link(src, dst, sem, dev, arrival=None):
        return pltpu.make_async_remote_copy(
            src_ref=src, dst_ref=dst, send_sem=ssem.at[sem],
            recv_sem=rsem.at[sem if arrival is None else arrival],
            device_id=dev, device_id_type=MESH,
        )

    fetches = [
        pltpu.make_async_copy(src, dst, lsem.at[n])
        for n, (src, dst) in enumerate([
            (vision_hbm.at[0], vision_ref.at[core]), (links_hbm, links_ref),
            (count_hbm, count_ref), (q_hbm, q_ref), (do_hbm, do_ref),
        ])
    ]
    for fetch in fetches:
        fetch.start()

    barrier = pltpu.get_barrier_semaphore()
    partners = (
        [partner]
        + [x_dev(k) for k in range(1, NX)]
        + [z_dev(k) for k in range(1, NZ)]
        + [y_dev(k, cc) for k in range(1, NY) for cc in (core, other)]
    )
    for dev in partners:
        pl.semaphore_signal(barrier, inc=1, device_id=dev, device_id_type=MESH)
    pl.semaphore_wait(barrier, len(partners))

    kind_here = lax.div(t, KVH)

    def w_slot(b, cc, low=0, size=HD):
        rows = pl.ds(pl.multiple_of(cc * HD + low, HD // 2), size)
        return w_all.at[lax.rem(b, KVH), rows, :]

    def w_copy(k):
        place = WG + (NY - k if k else 0) * 2
        return link(w_hbm, w_slot(t, core), place + core, y_dev(k, kind_here), place + core)

    def w_third(j, cc):
        slot = w_slot(lax.rem(t + j, NY), cc)
        up = j == 2
        return link(slot, slot, WG + (3 if up else 5) * 2 + cc, y_dev(NY - 1 if up else 1))

    def w_fourth(j, cc):
        up = j == 2
        slot = w_slot(lax.rem(t + j, NY), cc, 0 if up else HD // 2, HD // 2)
        return link(slot, slot, WG + (4 if up else 8) * 2 + cc, y_dev(NY - 2 if up else 2))

    vision_copy = link(vision_hbm.at[0], vision_ref.at[core], VS, partner)
    w_here = pltpu.make_async_copy(w_hbm, w_slot(t, core), lsem.at[5])
    near_w = (1, NY - 1, 2, NY - 2)

    for k in near_w:
        w_copy(k).start()

    @pl.when(kind_here == core)
    def _():
        w_here.start()

    @pl.when(kind_here != core)
    def _():
        w_copy(0).start()

    vision_copy.start()
    for fetch in fetches[:3]:
        fetch.wait()

    block = lax.broadcasted_iota(jnp.int32, links_ref.shape[1:], 1)
    slot = lax.broadcasted_iota(jnp.int32, (IMG_DOC, 1), 0)
    linked = jnp.sum(jnp.where(block == v, links_ref[0], 0), axis=1, keepdims=True)
    bias = jnp.where((linked == 1) & (slot < count_ref[...]), 0.0, -1e30)
    for s in range(IMG_DOC):
        bias_ref[s * IMG_LEN : (s + 1) * IMG_LEN, :] = jnp.broadcast_to(
            bias[s : s + 1, :], (IMG_LEN, HD)
        )

    class Sums:
        def __init__(self, base, xsend, xrecv, xown, zsend, zrecv, kv):
            self.base = base
            self.xsend, self.xrecv, self.xown = xsend, xrecv, xown
            self.zsend, self.zrecv, self.kv = zsend, zrecv, kv

        def x_copy(self, k):
            return link(self.xsend.at[k], self.xrecv.at[k], self.base + XS + k, x_dev(k))

        def z_copy(self, k):
            rows = piece(lax.rem(z + k, NZ))
            return link(self.zsend.at[rows, :], self.zrecv.at[k], self.base + ZS + k, z_dev(k))

        def az_copy(self, k, zz):
            ref = self.kv.at[mine, piece(zz), :]
            return link(ref, ref, self.base + AZ + k, z_dev(k))

        def ax_copy(self, k, h):
            ref = self.kv.at[core * KVH + h]
            return link(ref, ref, self.base + AX + k, x_dev(k))

        def across(self, i):
            h = lax.rem(x + i, NX)
            up = i == 1
            half = self.kv.at[core * KVH + h, pl.ds(0 if up else TOK // 2, TOK // 2), :]
            return link(half, half, self.base + AX + (2 if up else 4), x_dev(3 if up else 1))

        def ac_copy(self, kind, h):
            ref = self.kv.at[kind * KVH + h]
            return link(ref, ref, self.base + AC + h, partner)

        def x_step(self, h, total):
            k = lax.rem(h - x + NX, NX)

            @pl.when(k == 0)
            def _():
                self.xown[...] = total

            @pl.when(k != 0)
            def _():
                self.xsend[k] = total.astype(BF16)
                self.x_copy(k).start()

        def z_stage(self, first=lambda: None, second=lambda: None, share=False):
            total = self.xown[...]
            for k in near_first(NX):
                self.x_copy(k).wait_recv()
                total = total + self.xrecv[k].astype(F32)
            self.xown[...] = total
            self.zsend[...] = total.astype(BF16)
            for k in far_first(NZ):
                self.z_copy(k).start()
            first()
            part = self.xown[piece(z), :]
            for k in near_first(NZ):
                self.z_copy(k).wait_recv()
                part = part + self.zrecv[k].astype(F32)
            self.kv[mine, piece(z), :] = part.astype(BF16)
            for k in far_first(NZ):
                self.az_copy(k, z).start()
            second()
            for k in near_first(NZ):
                self.az_copy(k, lax.rem(z - k + NZ, NZ)).wait_recv()
            if share:
                self.ac_copy(core, x).start()
            for k in (1, 3):
                self.ax_copy(k, x).start()

        def x_arrive(self, i, share=False):
            h = lax.rem(x + i, NX)
            if i == 2:
                for place, low in ((2, 0), (4, TOK // 2)):
                    half = self.kv.at[core * KVH + h, pl.ds(low, TOK // 2), :]
                    link(half, half, self.base + AX + place, x_dev(1)).wait_recv()
            else:
                self.ax_copy(NX - i, h).wait_recv()
                self.across(i).start()
            if share:
                self.ac_copy(core, h).start()

        def partner_arrive(self, i):
            self.ac_copy(other, lax.rem(x + i, NX)).wait_recv()

        def sent(self):
            for k in range(1, NX):
                self.x_copy(k).wait_send()
            for k in (1, 3):
                self.ax_copy(k, x).wait_send()
                self.across(k).wait_send()
            for k in range(1, NZ):
                self.z_copy(k).wait_send()
                self.az_copy(k, z).wait_send()

    fwd = Sums(FWD, xsend1, xrecv1, xown1, zsend1, zrecv1, kv1)
    bwd = Sums(BWD, xsend2, xrecv2, xown2, zsend2, zrecv2, kv2)

    def near(n):
        far = lax.div(n + 1, 2)
        return jnp.where(lax.rem(n, 2) == 1, far, lax.rem(NY - far, NY))

    vision_copy.wait_recv()
    vt_ref[:HD, :] = vision_ref[0].T
    vt_ref[HD:, :] = vision_ref[1].T

    def w_loop(n, carry):
        j = near(n)
        b = lax.rem(t + j, NY)
        h = lax.rem(b, KVH)

        @pl.when(lax.div(b, KVH) == core)
        def _():
            @pl.when(j == 0)
            def _():
                w_here.wait()
                link(w_hbm, w_slot(b, other), WG + other, partner).wait_recv()

            for cc in range(2):
                @pl.when((j != 0) & (j != 4))
                def _():
                    link(w_hbm, w_slot(b, cc), WG + j * 2 + cc, partner).wait_recv()

                for hop in (2, 6):
                    @pl.when(j == hop)
                    def _():
                        w_third(hop, cc).start()
                        w_fourth(hop, cc).start()

                @pl.when(j == 4)
                def _():
                    for place, low in ((4, 0), (8, HD // 2)):
                        half = w_slot(b, cc, low, HD // 2)
                        link(half, half, WG + place * 2 + cc, partner).wait_recv()

            images = jnp.concatenate([vision_ref[0], vision_ref[1]], axis=1)
            part = jnp.dot(images, w_all[h], preferred_element_type=F32)
            fwd.x_step(h, part)

        return carry

    lax.fori_loop(0, NY, w_loop, 0)
    fwd.z_stage(share=True)

    for fetch in fetches[3:]:
        fetch.wait()

    def core_copy(h):
        return link(csend.at[h], crecv.at[h], BWD + CORE + h, partner)

    def head_step(h):
        core_copy(h).wait_recv()
        bwd.x_step(h, grads[h, core] + crecv[h].astype(F32))

    HALF = GROUP // 2

    def attend(u, carry):
        mine_now = (u == 0) | (u == 2 * KVH - 1)
        i = jnp.where(mine_now, 0, lax.div(u + 1, 2))
        half = jnp.where(mine_now, lax.div(u, 2 * KVH - 1), lax.rem(u + 1, 2))
        h = lax.rem(x + i, NX)
        base = h * GROUP * HD + half * HALF * HD

        def columns(j):
            return pl.ds(pl.multiple_of(base + j * HD, HD), HD)

        @pl.when(u == 1)
        def _():
            fwd.x_arrive(1, share=True)
            fwd.x_arrive(3, share=True)

        @pl.when(u == 2)
        def _():
            fwd.x_arrive(2, share=True)

        @pl.when(half == 0)
        def _():
            fwd.partner_arrive(i)

        dims = (((1,), (1,)), ((), ()))
        bias = jnp.concatenate([bias_ref[...]] * 2, axis=1)
        key_part = value_part = None
        for j in range(0, HALF, 2):
            q = jnp.concatenate([q_ref[:, columns(j)], q_ref[:, columns(j + 1)]], axis=0)
            do = jnp.concatenate([do_ref[:, columns(j)], do_ref[:, columns(j + 1)]], axis=0)
            s = lax.dot_general(kv1[h], q, dims, preferred_element_type=F32)
            g = lax.dot_general(kv1[KVH + h], do, dims, preferred_element_type=F32)
            s = s * (SCALE * LOG2E) + bias
            e = jnp.exp2(s - jnp.max(s, axis=0, keepdims=True))
            norm = 1.0 / jnp.sum(e, axis=0, keepdims=True)
            delta = jnp.sum(e * g, axis=0, keepdims=True) * norm
            probs = e * norm
            score_grad = (probs * (g - delta)).astype(BF16)
            place = pl.ds(pl.multiple_of((half * HALF + j) * HD, HD), 2 * HD)
            sg_ref[h, :, place] = score_grad
            key_more = jnp.dot(score_grad, q, preferred_element_type=F32)
            value_more = jnp.dot(probs.astype(BF16), do, preferred_element_type=F32)
            key_part = key_more if j == 0 else key_part + key_more
            value_part = value_more if j == 0 else value_part + value_more
        key_part = key_part * SCALE

        for when, done in ((3, 1), (5, 2), (7, 3)):
            @pl.when(u == when)
            def _():
                head_step(lax.rem(x + done, NX))

        @pl.when(half == 0)
        def _():
            grads[h, 0] = key_part
            grads[h, 1] = value_part

        @pl.when(half == 1)
        def _():
            grads[h, 0] += key_part
            grads[h, 1] += value_part
            csend[h] = grads[h, other].astype(BF16)
            core_copy(h).start()

        return carry

    lax.fori_loop(0, 2 * KVH, attend, 0)

    def query_grads(low, high):
        def one(i, carry):
            h = lax.rem(x + i, NX)
            dq = jnp.dot(kv1[h].T, sg_ref[h], preferred_element_type=F32) * SCALE
            for j in range(GROUP):
                place = pl.ds(pl.multiple_of((h * GROUP + j) * HD, HD), HD)
                dq_ref[:, place] = dq[:, j * HD : (j + 1) * HD].T.astype(BF16)
            return carry

        lax.fori_loop(low, high, one, 0)

    query_grads(0, 1)
    head_step(x)
    bwd.z_stage(lambda: query_grads(1, KVH))

    def y_copy(h, cc):
        k = lax.rem(core * KVH + h - t + NY, NY)
        return link(ysend.at[h, cc], yrecv.at[k], YS + h * 2 + cc, y_dev(k, cc), YS + k)

    images[...] = jnp.zeros((TOK, 2 * HD), F32)

    def y_loop(n, carry):
        i = jnp.where(n < 2, n, 5 - n)
        h = lax.rem(x + i, NX)
        b = core * KVH + h

        for when, place in ((1, 1), (2, 3), (3, 2)):
            @pl.when(n == when)
            def _():
                bwd.x_arrive(place)

        part = jnp.dot(vt_ref[...], kv2[b], preferred_element_type=F32)
        for cc in range(2):
            share = part[cc * HD : (cc + 1) * HD, :]

            @pl.when((b == t) & (core == cc))
            def _():
                yown[...] = share

            @pl.when((b != t) | (core != cc))
            def _():
                ysend[h, cc] = share.astype(BF16)
                y_copy(h, cc).start()

        images[...] += lax.dot_general(
            kv2[b], w_all[h], (((1,), (1,)), ((), ())), preferred_element_type=F32
        )
        return carry

    lax.fori_loop(0, KVH, y_loop, 0)

    vg_copy = link(vg_send, vg_recv, VG, partner)

    def half_of_images(first):
        low, high = images[:, :HD], images[:, HD:]
        return jnp.where(first == 0, low, high)

    vg_send[...] = half_of_images(other).astype(BF16)
    vg_copy.start()

    fwd.sent()
    bwd.sent()
    for h in range(KVH):
        fwd.ac_copy(core, h).wait_send()
        core_copy(h).wait_send()
    vision_copy.wait_send()
    for k in near_w:
        w_copy(k).wait_send()

    @pl.when(kind_here != core)
    def _():
        w_copy(0).wait_send()

    for hop in (2, 6):
        @pl.when(lax.div(lax.rem(t + hop, NY), KVH) == core)
        def _():
            for cc in range(2):
                w_third(hop, cc).wait_send()
                w_fourth(hop, cc).wait_send()

    vg_copy.wait_recv()
    vg_ref[0] = (half_of_images(core) + vg_recv[...].astype(F32)).astype(BF16)

    @pl.when(kind_here != core)
    def _():
        link(ysend.at[0, 0], yrecv.at[0], YS, partner).wait_recv()
        yown[...] = yrecv[0].astype(F32)

    grad = yown[...]
    for k in near_first(NY):
        link(ysend.at[0, 0], yrecv.at[k], YS + k, partner).wait_recv()
        grad = grad + yrecv[k].astype(F32)
    wg_ref[...] = grad
    vg_copy.wait_send()
    for h in range(KVH):
        for cc in range(2):
            @pl.when((core * KVH + h != t) | (core != cc))
            def _():
                y_copy(h, cc).wait_send()


def write(*refs):
    sources, targets, sem = refs[:3], refs[3:6], refs[6]
    copies = [
        pltpu.make_async_copy(src, dst, sem.at[n])
        for n, (src, dst) in enumerate(zip(sources, targets))
    ]
    for copy in copies:
        copy.start()
    for copy in copies:
        copy.wait()


def local(queries, out_grad, vision, w_kv, links, img_count):
    rows, width = queries.shape
    hbm = pl.BlockSpec(memory_space=pltpu.HBM)
    vmem = pl.BlockSpec(memory_space=pltpu.VMEM)
    sums = [
        pltpu.VMEM((NX, TOK, HD), BF16),
        pltpu.VMEM((NX, TOK, HD), BF16),
        pltpu.VMEM((TOK, HD), F32),
        pltpu.VMEM((TOK, HD), BF16),
        pltpu.VMEM((NZ, PIECE, HD), BF16),
        pltpu.VMEM((2 * KVH, TOK, HD), BF16),
    ]
    link_slots = jnp.swapaxes(links, 1, 2)
    out_shape = (
        pltpu.VMEM(queries.shape, BF16),
        pltpu.VMEM(vision.shape, BF16),
        pltpu.VMEM(w_kv.shape, F32),
    )
    results = pl.pallas_call(
        body,
        out_shape=out_shape,
        in_specs=[hbm] * 6,
        out_specs=(vmem, vmem, vmem),
        scratch_shapes=[
            pltpu.VMEM((rows, width), BF16),
            pltpu.VMEM((rows, width), BF16),
            pltpu.VMEM((2, TOK, HD), BF16),
            pltpu.VMEM(link_slots.shape, jnp.int32),
            pltpu.VMEM((1, 1), jnp.int32),
            pltpu.VMEM((TOK, HD), F32),
            pltpu.VMEM((2 * HD, TOK), BF16),
            pltpu.VMEM((KVH, 2 * HD, HD), BF16),
            pltpu.VMEM((TOK, HD), BF16),
            pltpu.VMEM((TOK, HD), BF16),
            pltpu.VMEM((KVH, TOK, GROUP * HD), BF16),
            pltpu.VMEM((KVH, 2, TOK, HD), F32),
            pltpu.VMEM((TOK, 2 * HD), F32),
            *sums,
            pltpu.VMEM((KVH, TOK, HD), BF16),
            pltpu.VMEM((KVH, TOK, HD), BF16),
            *sums,
            pltpu.VMEM((KVH, 2, HD, HD), BF16),
            pltpu.VMEM((NY, HD, HD), BF16),
            pltpu.VMEM((HD, HD), F32),
            pltpu.SemaphoreType.DMA((SEMS,)),
            pltpu.SemaphoreType.DMA((SEMS,)),
            pltpu.SemaphoreType.DMA((6,)),
        ],
        compiler_params=pltpu.CompilerParams(
            collective_id=0, has_side_effects=True, vmem_limit_bytes=40 * 1024 * 1024
        ),
    )(*[
        pltpu.with_memory_space_constraint(a, pltpu.HBM)
        for a in (queries, out_grad, vision, w_kv, link_slots)
    ], img_count.reshape(1, 1))
    return pl.pallas_call(
        write,
        out_shape=tuple(jax.ShapeDtypeStruct(r.shape, r.dtype) for r in results),
        in_specs=[vmem] * 3,
        out_specs=(hbm,) * 3,
        scratch_shapes=[pltpu.SemaphoreType.DMA((3,))],
    )(*results)


def solution(mesh):
    in_specs = (
        P(("txt", "vis"), None),
        P(("txt", "vis"), None),
        P("txt", None, "vis"),
        P("vis", "txt"),
        P("txt", None, None),
        P("txt"),
    )
    out_specs = (P(("txt", "vis"), None), P("txt", None, "vis"), P("vis", "txt"))
    return jax.shard_map(local, mesh=mesh, in_specs=in_specs, out_specs=out_specs, check_vma=False)
```

```python
import jax
import jax.numpy as jnp
from jax import lax
from jax.experimental import pallas as pl
from jax.experimental.pallas import tpu as pltpu
from jax.sharding import PartitionSpec as P

HD = 128
QH = 32
KVH = 4
GROUP = QH // KVH
IMG_DOC = 16
IMG_LEN = 24
TOK = IMG_DOC * IMG_LEN
NZ, NX, NY = 8, 4, 8
PIECE = TOK // NZ
SCALE = HD ** (-0.5)
LOG2E = 1.4426950408889634
MESH = pl.DeviceIdType.MESH
F32, BF16 = jnp.float32, jnp.bfloat16

CORE, XS, ZS, AZ, AX, AC = 0, 4, 8, 16, 24, 29
FWD, BWD, WG, YS, VS, VG = 0, 33, 66, 84, 92, 93
SEMS = 94


def near_first(n):
    return sorted(range(1, n), key=lambda k: min(k, n - k))


def far_first(n):
    return near_first(n)[::-1]


def body(
    q_hbm, do_hbm, vision_hbm, w_hbm, links_hbm, count_hbm,
    dq_ref, vg_ref, wg_ref,
    q_ref, do_ref, vision_ref, links_ref, count_ref, bias_ref, vt_ref, w_all, vg_send, vg_recv,
    sg_ref, grads, images,
    xsend1, xrecv1, xown1, zsend1, zrecv1, kv1,
    csend, crecv, xsend2, xrecv2, xown2, zsend2, zrecv2, kv2,
    ysend, yrecv, yown,
    ssem, rsem, lsem,
):
    v = lax.axis_index("vis")
    t = lax.axis_index("txt")
    core = lax.rem(v, 2)
    x = lax.rem(lax.div(v, 2), NX)
    z = lax.div(v, 2 * NX)
    other = 1 - core
    mine = core * KVH + x

    def vis_at(zz, xx, cc):
        return (zz * NX + xx) * 2 + cc

    partner = (vis_at(z, x, other), t)

    def x_dev(k):
        return (vis_at(z, lax.rem(x + k, NX), core), t)

    def z_dev(k):
        return (vis_at(lax.rem(z + k, NZ), x, core), t)

    def y_dev(k, cc=core):
        return (vis_at(z, x, cc), lax.rem(t + k, NY))

    def piece(zz):
        return pl.ds(pl.multiple_of(zz * PIECE, PIECE), PIECE)

    def link(src, dst, sem, dev, arrival=None):
        return pltpu.make_async_remote_copy(
            src_ref=src, dst_ref=dst, send_sem=ssem.at[sem],
            recv_sem=rsem.at[sem if arrival is None else arrival],
            device_id=dev, device_id_type=MESH,
        )

    fetches = [
        pltpu.make_async_copy(src, dst, lsem.at[n])
        for n, (src, dst) in enumerate([
            (vision_hbm.at[0], vision_ref.at[core]), (links_hbm, links_ref),
            (count_hbm, count_ref), (q_hbm, q_ref), (do_hbm, do_ref),
        ])
    ]
    for fetch in fetches:
        fetch.start()

    barrier = pltpu.get_barrier_semaphore()
    partners = (
        [y_dev(k, cc) for k in far_first(NY) for cc in (core, other)]
        + [z_dev(k) for k in far_first(NZ)]
        + [x_dev(k) for k in far_first(NX)]
        + [partner]
    )
    for dev in partners:
        pl.semaphore_signal(barrier, inc=1, device_id=dev, device_id_type=MESH)
    pl.semaphore_wait(barrier, len(partners))

    kind_here = lax.div(t, KVH)

    def w_slot(b, cc, low=0, size=HD):
        rows = pl.ds(pl.multiple_of(cc * HD + low, HD // 2), size)
        return w_all.at[lax.rem(b, KVH), rows, :]

    def w_copy(k):
        place = WG + (NY - k if k else 0) * 2
        return link(w_hbm, w_slot(t, core), place + core, y_dev(k, kind_here), place + core)

    def w_third(j, cc):
        slot = w_slot(lax.rem(t + j, NY), cc)
        up = j == 2
        return link(slot, slot, WG + (3 if up else 5) * 2 + cc, y_dev(NY - 1 if up else 1))

    def w_fourth(j, cc):
        up = j == 2
        slot = w_slot(lax.rem(t + j, NY), cc, 0 if up else HD // 2, HD // 2)
        return link(slot, slot, WG + (4 if up else 8) * 2 + cc, y_dev(NY - 2 if up else 2))

    vision_copy = link(vision_hbm.at[0], vision_ref.at[core], VS, partner)
    w_here = pltpu.make_async_copy(w_hbm, w_slot(t, core), lsem.at[5])
    near_w = (1, NY - 1, 2, NY - 2)

    for k in near_w:
        w_copy(k).start()

    @pl.when(kind_here == core)
    def _():
        w_here.start()

    @pl.when(kind_here != core)
    def _():
        w_copy(0).start()

    vision_copy.start()
    for fetch in fetches[:3]:
        fetch.wait()

    block = lax.broadcasted_iota(jnp.int32, links_ref.shape[1:], 1)
    slot = lax.broadcasted_iota(jnp.int32, (IMG_DOC, 1), 0)
    linked = jnp.sum(jnp.where(block == v, links_ref[0], 0), axis=1, keepdims=True)
    bias = jnp.where((linked == 1) & (slot < count_ref[...]), 0.0, -1e30)
    for s in range(IMG_DOC):
        bias_ref[s * IMG_LEN : (s + 1) * IMG_LEN, :] = jnp.broadcast_to(
            bias[s : s + 1, :], (IMG_LEN, HD)
        )

    class Sums:
        def __init__(self, base, xsend, xrecv, xown, zsend, zrecv, kv):
            self.base = base
            self.xsend, self.xrecv, self.xown = xsend, xrecv, xown
            self.zsend, self.zrecv, self.kv = zsend, zrecv, kv

        def x_copy(self, k):
            return link(self.xsend.at[k], self.xrecv.at[k], self.base + XS + k, x_dev(k))

        def z_copy(self, k):
            rows = piece(lax.rem(z + k, NZ))
            return link(self.zsend.at[rows, :], self.zrecv.at[k], self.base + ZS + k, z_dev(k))

        def az_copy(self, k, zz):
            ref = self.kv.at[mine, piece(zz), :]
            return link(ref, ref, self.base + AZ + k, z_dev(k))

        def ax_copy(self, k, h):
            ref = self.kv.at[core * KVH + h]
            return link(ref, ref, self.base + AX + k, x_dev(k))

        def across(self, i):
            h = lax.rem(x + i, NX)
            up = i == 1
            half = self.kv.at[core * KVH + h, pl.ds(0 if up else TOK // 2, TOK // 2), :]
            return link(half, half, self.base + AX + (2 if up else 4), x_dev(3 if up else 1))

        def ac_copy(self, kind, h):
            ref = self.kv.at[kind * KVH + h]
            return link(ref, ref, self.base + AC + h, partner)

        def x_step(self, h, total):
            k = lax.rem(h - x + NX, NX)

            @pl.when(k == 0)
            def _():
                self.xown[...] = total

            @pl.when(k != 0)
            def _():
                self.xsend[k] = total.astype(BF16)
                self.x_copy(k).start()

        def z_stage(self, first=lambda: None, second=lambda: None, share=False):
            total = self.xown[...]
            for k in near_first(NX):
                self.x_copy(k).wait_recv()
                total = total + self.xrecv[k].astype(F32)
            self.xown[...] = total
            self.zsend[...] = total.astype(BF16)
            for k in far_first(NZ):
                self.z_copy(k).start()
            first()
            part = self.xown[piece(z), :]
            for k in near_first(NZ):
                self.z_copy(k).wait_recv()
                part = part + self.zrecv[k].astype(F32)
            self.kv[mine, piece(z), :] = part.astype(BF16)
            for k in far_first(NZ):
                self.az_copy(k, z).start()
            second()
            for k in near_first(NZ):
                self.az_copy(k, lax.rem(z - k + NZ, NZ)).wait_recv()
            if share:
                self.ac_copy(core, x).start()
            for k in (1, 3):
                self.ax_copy(k, x).start()

        def x_arrive(self, i, share=False):
            h = lax.rem(x + i, NX)
            if i == 2:
                for place, low in ((2, 0), (4, TOK // 2)):
                    half = self.kv.at[core * KVH + h, pl.ds(low, TOK // 2), :]
                    link(half, half, self.base + AX + place, x_dev(1)).wait_recv()
            else:
                self.ax_copy(NX - i, h).wait_recv()
                self.across(i).start()
            if share:
                self.ac_copy(core, h).start()

        def partner_arrive(self, i):
            self.ac_copy(other, lax.rem(x + i, NX)).wait_recv()

        def sent(self):
            for k in range(1, NX):
                self.x_copy(k).wait_send()
            for k in (1, 3):
                self.ax_copy(k, x).wait_send()
                self.across(k).wait_send()
            for k in range(1, NZ):
                self.z_copy(k).wait_send()
                self.az_copy(k, z).wait_send()

    fwd = Sums(FWD, xsend1, xrecv1, xown1, zsend1, zrecv1, kv1)
    bwd = Sums(BWD, xsend2, xrecv2, xown2, zsend2, zrecv2, kv2)

    def near(n):
        far = lax.div(n + 1, 2)
        return jnp.where(lax.rem(n, 2) == 1, far, lax.rem(NY - far, NY))

    vision_copy.wait_recv()
    vt_ref[:HD, :] = vision_ref[0].T
    vt_ref[HD:, :] = vision_ref[1].T

    def w_loop(n, carry):
        j = near(n)
        b = lax.rem(t + j, NY)
        h = lax.rem(b, KVH)

        @pl.when(lax.div(b, KVH) == core)
        def _():
            @pl.when(j == 0)
            def _():
                w_here.wait()
                link(w_hbm, w_slot(b, other), WG + other, partner).wait_recv()

            for cc in range(2):
                @pl.when((j != 0) & (j != 4))
                def _():
                    link(w_hbm, w_slot(b, cc), WG + j * 2 + cc, partner).wait_recv()

                for hop in (2, 6):
                    @pl.when(j == hop)
                    def _():
                        w_third(hop, cc).start()
                        w_fourth(hop, cc).start()

                @pl.when(j == 4)
                def _():
                    for place, low in ((4, 0), (8, HD // 2)):
                        half = w_slot(b, cc, low, HD // 2)
                        link(half, half, WG + place * 2 + cc, partner).wait_recv()

            images = jnp.concatenate([vision_ref[0], vision_ref[1]], axis=1)
            part = jnp.dot(images, w_all[h], preferred_element_type=F32)
            fwd.x_step(h, part)

        return carry

    lax.fori_loop(0, NY, w_loop, 0)
    fwd.z_stage(share=True)

    for fetch in fetches[3:]:
        fetch.wait()

    def core_copy(h):
        return link(csend.at[h], crecv.at[h], BWD + CORE + h, partner)

    def head_step(h):
        core_copy(h).wait_recv()
        bwd.x_step(h, grads[h, core] + crecv[h].astype(F32))

    HALF = GROUP // 2

    def attend(u, carry):
        mine_now = (u == 0) | (u == 2 * KVH - 1)
        i = jnp.where(mine_now, 0, lax.div(u + 1, 2))
        half = jnp.where(mine_now, lax.div(u, 2 * KVH - 1), lax.rem(u + 1, 2))
        h = lax.rem(x + i, NX)
        base = h * GROUP * HD + half * HALF * HD

        def columns(j):
            return pl.ds(pl.multiple_of(base + j * HD, HD), HD)

        @pl.when(u == 1)
        def _():
            fwd.x_arrive(1, share=True)
            fwd.x_arrive(3, share=True)

        @pl.when(u == 2)
        def _():
            fwd.x_arrive(2, share=True)

        @pl.when(half == 0)
        def _():
            fwd.partner_arrive(i)

        dims = (((1,), (1,)), ((), ()))
        bias = jnp.concatenate([bias_ref[...]] * 2, axis=1)
        key_part = value_part = None
        for j in range(0, HALF, 2):
            q = jnp.concatenate([q_ref[:, columns(j)], q_ref[:, columns(j + 1)]], axis=0)
            do = jnp.concatenate([do_ref[:, columns(j)], do_ref[:, columns(j + 1)]], axis=0)
            s = lax.dot_general(kv1[h], q, dims, preferred_element_type=F32)
            g = lax.dot_general(kv1[KVH + h], do, dims, preferred_element_type=F32)
            s = s * (SCALE * LOG2E) + bias
            e = jnp.exp2(s - jnp.max(s, axis=0, keepdims=True))
            norm = 1.0 / jnp.sum(e, axis=0, keepdims=True)
            delta = jnp.sum(e * g, axis=0, keepdims=True) * norm
            probs = e * norm
            score_grad = (probs * (g - delta)).astype(BF16)
            place = pl.ds(pl.multiple_of((half * HALF + j) * HD, HD), 2 * HD)
            sg_ref[h, :, place] = score_grad
            key_more = jnp.dot(score_grad, q, preferred_element_type=F32)
            value_more = jnp.dot(probs.astype(BF16), do, preferred_element_type=F32)
            key_part = key_more if j == 0 else key_part + key_more
            value_part = value_more if j == 0 else value_part + value_more
        key_part = key_part * SCALE

        for when, done in ((3, 1), (5, 2), (7, 3)):
            @pl.when(u == when)
            def _():
                head_step(lax.rem(x + done, NX))

        @pl.when(half == 0)
        def _():
            grads[h, 0] = key_part
            grads[h, 1] = value_part

        @pl.when(half == 1)
        def _():
            grads[h, 0] += key_part
            grads[h, 1] += value_part
            csend[h] = grads[h, other].astype(BF16)
            core_copy(h).start()

        return carry

    lax.fori_loop(0, 2 * KVH, attend, 0)

    def query_grads(low, high):
        def one(i, carry):
            h = lax.rem(x + i, NX)
            dq = jnp.dot(kv1[h].T, sg_ref[h], preferred_element_type=F32) * SCALE
            for j in range(GROUP):
                place = pl.ds(pl.multiple_of((h * GROUP + j) * HD, HD), HD)
                dq_ref[:, place] = dq[:, j * HD : (j + 1) * HD].T.astype(BF16)
            return carry

        lax.fori_loop(low, high, one, 0)

    ahead = 2 * core
    query_grads(0, ahead)
    head_step(x)
    bwd.z_stage(lambda: query_grads(ahead, KVH))

    def y_copy(h, cc):
        k = lax.rem(core * KVH + h - t + NY, NY)
        return link(ysend.at[h, cc], yrecv.at[k], YS + h * 2 + cc, y_dev(k, cc), YS + k)

    images[...] = jnp.zeros((TOK, 2 * HD), F32)

    def y_loop(n, carry):
        i = jnp.where(n < 2, n, 5 - n)
        h = lax.rem(x + i, NX)
        b = core * KVH + h

        for when, place in ((1, 1), (2, 3), (3, 2)):
            @pl.when(n == when)
            def _():
                bwd.x_arrive(place)

        part = jnp.dot(vt_ref[...], kv2[b], preferred_element_type=F32)
        for cc in range(2):
            share = part[cc * HD : (cc + 1) * HD, :]

            @pl.when((b == t) & (core == cc))
            def _():
                yown[...] = share

            @pl.when((b != t) | (core != cc))
            def _():
                ysend[h, cc] = share.astype(BF16)
                y_copy(h, cc).start()

        images[...] += lax.dot_general(
            kv2[b], w_all[h], (((1,), (1,)), ((), ())), preferred_element_type=F32
        )
        return carry

    lax.fori_loop(0, KVH, y_loop, 0)

    vg_copy = link(vg_send, vg_recv, VG, partner)

    def half_of_images(first):
        low, high = images[:, :HD], images[:, HD:]
        return jnp.where(first == 0, low, high)

    vg_send[...] = half_of_images(other).astype(BF16)
    vg_copy.start()

    fwd.sent()
    bwd.sent()
    for h in range(KVH):
        fwd.ac_copy(core, h).wait_send()
        core_copy(h).wait_send()
    vision_copy.wait_send()
    for k in near_w:
        w_copy(k).wait_send()

    @pl.when(kind_here != core)
    def _():
        w_copy(0).wait_send()

    for hop in (2, 6):
        @pl.when(lax.div(lax.rem(t + hop, NY), KVH) == core)
        def _():
            for cc in range(2):
                w_third(hop, cc).wait_send()
                w_fourth(hop, cc).wait_send()

    vg_copy.wait_recv()
    vg_ref[0] = (half_of_images(core) + vg_recv[...].astype(F32)).astype(BF16)

    @pl.when(kind_here != core)
    def _():
        link(ysend.at[0, 0], yrecv.at[0], YS, partner).wait_recv()
        yown[...] = yrecv[0].astype(F32)

    grad = yown[...]
    for k in near_first(NY):
        link(ysend.at[0, 0], yrecv.at[k], YS + k, partner).wait_recv()
        grad = grad + yrecv[k].astype(F32)
    wg_ref[...] = grad
    vg_copy.wait_send()
    for h in range(KVH):
        for cc in range(2):
            @pl.when((core * KVH + h != t) | (core != cc))
            def _():
                y_copy(h, cc).wait_send()


def write(*refs):
    sources, targets, sem = refs[:3], refs[3:6], refs[6]
    copies = [
        pltpu.make_async_copy(src, dst, sem.at[n])
        for n, (src, dst) in enumerate(zip(sources, targets))
    ]
    for copy in copies:
        copy.start()
    for copy in copies:
        copy.wait()


def local(queries, out_grad, vision, w_kv, links, img_count):
    rows, width = queries.shape
    hbm = pl.BlockSpec(memory_space=pltpu.HBM)
    vmem = pl.BlockSpec(memory_space=pltpu.VMEM)
    sums = [
        pltpu.VMEM((NX, TOK, HD), BF16),
        pltpu.VMEM((NX, TOK, HD), BF16),
        pltpu.VMEM((TOK, HD), F32),
        pltpu.VMEM((TOK, HD), BF16),
        pltpu.VMEM((NZ, PIECE, HD), BF16),
        pltpu.VMEM((2 * KVH, TOK, HD), BF16),
    ]
    link_slots = jnp.swapaxes(links, 1, 2)
    out_shape = (
        pltpu.VMEM(queries.shape, BF16),
        pltpu.VMEM(vision.shape, BF16),
        pltpu.VMEM(w_kv.shape, F32),
    )
    results = pl.pallas_call(
        body,
        out_shape=out_shape,
        in_specs=[hbm] * 6,
        out_specs=(vmem, vmem, vmem),
        scratch_shapes=[
            pltpu.VMEM((rows, width), BF16),
            pltpu.VMEM((rows, width), BF16),
            pltpu.VMEM((2, TOK, HD), BF16),
            pltpu.VMEM(link_slots.shape, jnp.int32),
            pltpu.VMEM((1, 1), jnp.int32),
            pltpu.VMEM((TOK, HD), F32),
            pltpu.VMEM((2 * HD, TOK), BF16),
            pltpu.VMEM((KVH, 2 * HD, HD), BF16),
            pltpu.VMEM((TOK, HD), BF16),
            pltpu.VMEM((TOK, HD), BF16),
            pltpu.VMEM((KVH, TOK, GROUP * HD), BF16),
            pltpu.VMEM((KVH, 2, TOK, HD), F32),
            pltpu.VMEM((TOK, 2 * HD), F32),
            *sums,
            pltpu.VMEM((KVH, TOK, HD), BF16),
            pltpu.VMEM((KVH, TOK, HD), BF16),
            *sums,
            pltpu.VMEM((KVH, 2, HD, HD), BF16),
            pltpu.VMEM((NY, HD, HD), BF16),
            pltpu.VMEM((HD, HD), F32),
            pltpu.SemaphoreType.DMA((SEMS,)),
            pltpu.SemaphoreType.DMA((SEMS,)),
            pltpu.SemaphoreType.DMA((6,)),
        ],
        compiler_params=pltpu.CompilerParams(
            collective_id=0, has_side_effects=True, vmem_limit_bytes=40 * 1024 * 1024
        ),
    )(*[
        pltpu.with_memory_space_constraint(a, pltpu.HBM)
        for a in (queries, out_grad, vision, w_kv, link_slots)
    ], img_count.reshape(1, 1))
    return pl.pallas_call(
        write,
        out_shape=tuple(jax.ShapeDtypeStruct(r.shape, r.dtype) for r in results),
        in_specs=[vmem] * 3,
        out_specs=(hbm,) * 3,
        scratch_shapes=[pltpu.SemaphoreType.DMA((3,))],
        compiler_params=pltpu.CompilerParams(vmem_limit_bytes=4 * 1024 * 1024),
    )(*[pltpu.with_memory_space_constraint(a, pltpu.VMEM) for a in results])


def solution(mesh):
    in_specs = (
        P(("txt", "vis"), None),
        P(("txt", "vis"), None),
        P("txt", None, "vis"),
        P("vis", "txt"),
        P("txt", None, None),
        P("txt"),
    )
    out_specs = (P(("txt", "vis"), None), P("txt", None, "vis"), P("vis", "txt"))
    return jax.shard_map(local, mesh=mesh, in_specs=in_specs, out_specs=out_specs, check_vma=False)
```

```python
import jax
import jax.numpy as jnp
from jax import lax
from jax.experimental import pallas as pl
from jax.experimental.pallas import tpu as pltpu
from jax.sharding import PartitionSpec as P

HD = 128
QH = 32
KVH = 4
GROUP = QH // KVH
IMG_DOC = 16
IMG_LEN = 24
TOK = IMG_DOC * IMG_LEN
NZ, NX, NY = 8, 4, 8
PIECE = TOK // NZ
SCALE = HD ** (-0.5)
LOG2E = 1.4426950408889634
MESH = pl.DeviceIdType.MESH
F32, BF16 = jnp.float32, jnp.bfloat16

CORE, XS, ZS, AZ, AX, AC, XZ = 0, 4, 8, 16, 24, 30, 34
FWD, BWD, WG, YS, VS, VG = 0, 42, 84, 102, 110, 111
SEMS = 112


def near_first(n):
    return sorted(range(1, n), key=lambda k: min(k, n - k))


def far_first(n):
    return near_first(n)[::-1]


def body(
    q_hbm, do_hbm, vision_hbm, w_hbm, links_hbm, count_hbm,
    dq_ref, vg_ref, wg_ref,
    q_ref, do_ref, vision_ref, links_ref, count_ref, bias_ref, vt_ref, w_all, vg_send, vg_recv,
    sg_ref, grads, images,
    xsend1, xrecv1, xown1, zsend1, zrecv1, kv1,
    csend, crecv, xsend2, xrecv2, xown2, zsend2, zrecv2, kv2,
    xz_recv, ysend, yrecv, yown,
    ssem, rsem, lsem,
):
    v = lax.axis_index("vis")
    t = lax.axis_index("txt")
    core = lax.rem(v, 2)
    x = lax.rem(lax.div(v, 2), NX)
    z = lax.div(v, 2 * NX)
    other = 1 - core
    mine = core * KVH + x

    def vis_at(zz, xx, cc):
        return (zz * NX + xx) * 2 + cc

    partner = (vis_at(z, x, other), t)

    def x_dev(k):
        return (vis_at(z, lax.rem(x + k, NX), core), t)

    def z_dev(k):
        return (vis_at(lax.rem(z + k, NZ), x, core), t)

    def xz_dev(i, k):
        return (vis_at(lax.rem(z + k, NZ), lax.rem(x + i, NX), core), t)

    def y_dev(k, cc=core):
        return (vis_at(z, x, cc), lax.rem(t + k, NY))

    def piece(zz):
        return pl.ds(pl.multiple_of(zz * PIECE, PIECE), PIECE)

    def link(src, dst, sem, dev, arrival=None):
        return pltpu.make_async_remote_copy(
            src_ref=src, dst_ref=dst, send_sem=ssem.at[sem],
            recv_sem=rsem.at[sem if arrival is None else arrival],
            device_id=dev, device_id_type=MESH,
        )

    fetches = [
        pltpu.make_async_copy(src, dst, lsem.at[n])
        for n, (src, dst) in enumerate([
            (vision_hbm.at[0], vision_ref.at[core]), (links_hbm, links_ref),
            (count_hbm, count_ref), (q_hbm, q_ref), (do_hbm, do_ref),
        ])
    ]
    for fetch in fetches:
        fetch.start()

    barrier = pltpu.get_barrier_semaphore()
    partners = (
        [y_dev(k, cc) for k in far_first(NY) for cc in (core, other)]
        + [z_dev(k) for k in far_first(NZ)]
        + [x_dev(k) for k in far_first(NX)]
        + [partner]
        + [xz_dev(1, k) for k in range(1, NZ)]
    )
    for dev in partners:
        pl.semaphore_signal(barrier, inc=1, device_id=dev, device_id_type=MESH)
    pl.semaphore_wait(barrier, len(partners))

    kind_here = lax.div(t, KVH)

    def w_slot(b, cc, low=0, size=HD):
        rows = pl.ds(pl.multiple_of(cc * HD + low, HD // 2), size)
        return w_all.at[lax.rem(b, KVH), rows, :]

    def w_copy(k):
        place = WG + (NY - k if k else 0) * 2
        return link(w_hbm, w_slot(t, core), place + core, y_dev(k, kind_here), place + core)

    def w_third(j, cc):
        slot = w_slot(lax.rem(t + j, NY), cc)
        up = j == 2
        return link(slot, slot, WG + (3 if up else 5) * 2 + cc, y_dev(NY - 1 if up else 1))

    def w_fourth(j, cc):
        up = j == 2
        slot = w_slot(lax.rem(t + j, NY), cc, 0 if up else HD // 2, HD // 2)
        return link(slot, slot, WG + (4 if up else 8) * 2 + cc, y_dev(NY - 2 if up else 2))

    vision_copy = link(vision_hbm.at[0], vision_ref.at[core], VS, partner)
    w_here = pltpu.make_async_copy(w_hbm, w_slot(t, core), lsem.at[5])
    near_w = (1, NY - 1, 2, NY - 2)

    for k in near_w:
        w_copy(k).start()

    @pl.when(kind_here == core)
    def _():
        w_here.start()

    @pl.when(kind_here != core)
    def _():
        w_copy(0).start()

    vision_copy.start()
    for fetch in fetches[:3]:
        fetch.wait()

    block = lax.broadcasted_iota(jnp.int32, links_ref.shape[1:], 1)
    slot = lax.broadcasted_iota(jnp.int32, (IMG_DOC, 1), 0)
    linked = jnp.sum(jnp.where(block == v, links_ref[0], 0), axis=1, keepdims=True)
    bias = jnp.where((linked == 1) & (slot < count_ref[...]), 0.0, -1e30)
    for s in range(IMG_DOC):
        bias_ref[s * IMG_LEN : (s + 1) * IMG_LEN, :] = jnp.broadcast_to(
            bias[s : s + 1, :], (IMG_LEN, HD)
        )

    class Sums:
        def __init__(self, base, xsend, xrecv, xown, zsend, zrecv, kv):
            self.base = base
            self.xsend, self.xrecv, self.xown = xsend, xrecv, xown
            self.zsend, self.zrecv, self.kv = zsend, zrecv, kv

        def x_copy(self, k):
            return link(self.xsend.at[k], self.xrecv.at[k], self.base + XS + k, x_dev(k))

        def z_copy(self, k):
            rows = piece(lax.rem(z + k, NZ))
            return link(self.zsend.at[rows, :], self.zrecv.at[k], self.base + ZS + k, z_dev(k))

        def az_copy(self, k, zz):
            ref = self.kv.at[mine, piece(zz), :]
            return link(ref, ref, self.base + AZ + k, z_dev(k))

        def half_block(self, h, part):
            return self.kv.at[core * KVH + h, pl.ds(part * (TOK // 2), TOK // 2), :]

        def ax_copy(self, k, h, part):
            half = self.half_block(h, part)
            return link(half, half, self.base + AX + (k - 1) + part, x_dev(k))

        def across(self, i):
            part = 0 if i == 1 else 1
            half = self.half_block(lax.rem(x + i, NX), part)
            return link(half, half, self.base + AX + 4 + part, x_dev(NX - i))

        def ac_copy(self, kind, h):
            ref = self.kv.at[kind * KVH + h]
            return link(ref, ref, self.base + AC + h, partner)

        def x_step(self, h, total):
            k = lax.rem(h - x + NX, NX)

            @pl.when(k == 0)
            def _():
                self.xown[...] = total

            @pl.when(k != 0)
            def _():
                self.xsend[k] = total.astype(BF16)
                self.x_copy(k).start()

        def z_stage(self, first=lambda: None, share=False, from_x=(1, 3, 2), more=lambda part: part):
            total = self.xown[...]
            for k in from_x:
                self.x_copy(k).wait_recv()
                total = total + self.xrecv[k].astype(F32)
            self.xown[...] = total
            self.zsend[...] = total.astype(BF16)
            for k in far_first(NZ):
                self.z_copy(k).start()
            first()
            part = self.xown[piece(z), :]
            for k in near_first(NZ):
                self.z_copy(k).wait_recv()
                part = part + self.zrecv[k].astype(F32)
            self.kv[mine, piece(z), :] = more(part).astype(BF16)
            for k in far_first(NZ):
                self.az_copy(k, z).start()
            for k in near_first(NZ):
                self.az_copy(k, lax.rem(z - k + NZ, NZ)).wait_recv()
            if share:
                self.ac_copy(core, x).start()
            for k, half in ((3, 0), (1, 1), (3, 1), (1, 0)):
                self.ax_copy(k, x, half).start()

        def pass_on(self, i):
            h = lax.rem(x + i, NX)
            self.ax_copy(NX - i, h, 0 if i == 1 else 1).wait_recv()
            self.across(i).start()

        def x_arrive(self, i, share=False):
            h = lax.rem(x + i, NX)
            if i == 2:
                for part in range(2):
                    half = self.half_block(h, part)
                    link(half, half, self.base + AX + 4 + part, x_dev(1)).wait_recv()
            else:
                self.ax_copy(NX - i, h, 1 if i == 1 else 0).wait_recv()
            if share:
                self.ac_copy(core, h).start()

        def partner_arrive(self, i):
            self.ac_copy(other, lax.rem(x + i, NX)).wait_recv()

        def sent(self, to_x=(1, 2, 3)):
            for k in to_x:
                self.x_copy(k).wait_send()
            for k in (1, 3):
                for part in range(2):
                    self.ax_copy(k, x, part).wait_send()
                self.across(k).wait_send()
            for k in range(1, NZ):
                self.z_copy(k).wait_send()
                self.az_copy(k, z).wait_send()

    fwd = Sums(FWD, xsend1, xrecv1, xown1, zsend1, zrecv1, kv1)
    bwd = Sums(BWD, xsend2, xrecv2, xown2, zsend2, zrecv2, kv2)

    def near(n):
        far = lax.div(n + 1, 2)
        return jnp.where(lax.rem(n, 2) == 1, far, lax.rem(NY - far, NY))

    vision_copy.wait_recv()
    vt_ref[:HD, :] = vision_ref[0].T
    vt_ref[HD:, :] = vision_ref[1].T

    def w_loop(n, carry):
        j = near(n)
        b = lax.rem(t + j, NY)
        h = lax.rem(b, KVH)

        @pl.when(lax.div(b, KVH) == core)
        def _():
            @pl.when(j == 0)
            def _():
                w_here.wait()
                link(w_hbm, w_slot(b, other), WG + other, partner).wait_recv()

            for cc in range(2):
                @pl.when((j != 0) & (j != 4))
                def _():
                    link(w_hbm, w_slot(b, cc), WG + j * 2 + cc, partner).wait_recv()

                for hop in (2, 6):
                    @pl.when(j == hop)
                    def _():
                        w_third(hop, cc).start()
                        w_fourth(hop, cc).start()

                @pl.when(j == 4)
                def _():
                    for place, low in ((4, 0), (8, HD // 2)):
                        half = w_slot(b, cc, low, HD // 2)
                        link(half, half, WG + place * 2 + cc, partner).wait_recv()

            images = jnp.concatenate([vision_ref[0], vision_ref[1]], axis=1)
            part = jnp.dot(images, w_all[h], preferred_element_type=F32)
            fwd.x_step(h, part)

        return carry

    lax.fori_loop(0, NY, w_loop, 0)
    fwd.z_stage(share=True)

    for fetch in fetches[3:]:
        fetch.wait()

    def core_copy(h):
        return link(csend.at[h], crecv.at[h], BWD + CORE + h, partner)

    def xz_copy(k):
        rows = piece(lax.rem(z + k, NZ))
        return link(xsend2.at[3, rows, :], xz_recv.at[k], BWD + XZ + k, xz_dev(3, k))

    def last_step():
        h = lax.rem(x + 3, NX)
        core_copy(h).wait_recv()
        xsend2[3] = (grads[h, core] + crecv[h].astype(F32)).astype(BF16)
        for k in [*far_first(NZ), 0]:
            xz_copy(k).start()

    def last_arrive(part):
        for k in [0, *near_first(NZ)]:
            xz_copy(k).wait_recv()
            part = part + xz_recv[k].astype(F32)
        return part

    def head_step(h):
        core_copy(h).wait_recv()
        bwd.x_step(h, grads[h, core] + crecv[h].astype(F32))

    HALF = GROUP // 2

    def attend(u, carry):
        mine_now = (u == 0) | (u == 2 * KVH - 1)
        i = jnp.where(mine_now, 0, lax.div(u + 1, 2))
        half = jnp.where(mine_now, lax.div(u, 2 * KVH - 1), lax.rem(u + 1, 2))
        h = lax.rem(x + i, NX)
        base = h * GROUP * HD + half * HALF * HD

        def columns(j):
            return pl.ds(pl.multiple_of(base + j * HD, HD), HD)

        @pl.when(u == 1)
        def _():
            fwd.pass_on(1)
            fwd.pass_on(3)
            fwd.x_arrive(1, share=True)
            fwd.x_arrive(3, share=True)

        @pl.when(u == 2)
        def _():
            fwd.x_arrive(2, share=True)

        @pl.when(half == 0)
        def _():
            fwd.partner_arrive(i)

        dims = (((1,), (1,)), ((), ()))
        bias = jnp.concatenate([bias_ref[...]] * 2, axis=1)
        key_part = value_part = None
        for j in range(0, HALF, 2):
            q = jnp.concatenate([q_ref[:, columns(j)], q_ref[:, columns(j + 1)]], axis=0)
            do = jnp.concatenate([do_ref[:, columns(j)], do_ref[:, columns(j + 1)]], axis=0)
            s = lax.dot_general(kv1[h], q, dims, preferred_element_type=F32)
            g = lax.dot_general(kv1[KVH + h], do, dims, preferred_element_type=F32)
            s = s * (SCALE * LOG2E) + bias
            e = jnp.exp2(s - jnp.max(s, axis=0, keepdims=True))
            norm = 1.0 / jnp.sum(e, axis=0, keepdims=True)
            delta = jnp.sum(e * g, axis=0, keepdims=True) * norm
            probs = e * norm
            score_grad = (probs * (g - delta)).astype(BF16)
            place = pl.ds(pl.multiple_of((half * HALF + j) * HD, HD), 2 * HD)
            sg_ref[h, :, place] = score_grad
            key_more = jnp.dot(score_grad, q, preferred_element_type=F32)
            value_more = jnp.dot(probs.astype(BF16), do, preferred_element_type=F32)
            key_part = key_more if j == 0 else key_part + key_more
            value_part = value_more if j == 0 else value_part + value_more
        key_part = key_part * SCALE

        @pl.when(half == 0)
        def _():
            grads[h, 0] = key_part
            grads[h, 1] = value_part

        @pl.when(half == 1)
        def _():
            grads[h, 0] += key_part
            grads[h, 1] += value_part
            csend[h] = grads[h, other].astype(BF16)
            core_copy(h).start()

        for when, done in ((3, 1), (5, 2)):
            @pl.when(u == when)
            def _():
                head_step(lax.rem(x + done, NX))

        return carry

    lax.fori_loop(0, 2 * KVH, attend, 0)
    last_step()

    def query_grads(low, high):
        def one(i, carry):
            h = lax.rem(x + i, NX)
            dq = jnp.dot(kv1[h].T, sg_ref[h], preferred_element_type=F32) * SCALE
            for j in range(GROUP):
                place = pl.ds(pl.multiple_of((h * GROUP + j) * HD, HD), HD)
                dq_ref[:, place] = dq[:, j * HD : (j + 1) * HD].T.astype(BF16)
            return carry

        lax.fori_loop(low, high, one, 0)

    query_grads(0, 1)
    head_step(x)
    bwd.z_stage(lambda: query_grads(1, KVH), from_x=(1, 2), more=last_arrive)

    def y_copy(h, cc):
        k = lax.rem(core * KVH + h - t + NY, NY)
        return link(ysend.at[h, cc], yrecv.at[k], YS + h * 2 + cc, y_dev(k, cc), YS + k)

    images[...] = jnp.zeros((TOK, 2 * HD), F32)

    def y_loop(n, carry):
        i = jnp.where(n < 2, n, 5 - n)
        h = lax.rem(x + i, NX)
        b = core * KVH + h

        @pl.when(n == 1)
        def _():
            bwd.pass_on(1)
            bwd.pass_on(3)

        for when, place in ((1, 1), (2, 3), (3, 2)):
            @pl.when(n == when)
            def _():
                bwd.x_arrive(place)

        part = jnp.dot(vt_ref[...], kv2[b], preferred_element_type=F32)
        for cc in range(2):
            share = part[cc * HD : (cc + 1) * HD, :]

            @pl.when((b == t) & (core == cc))
            def _():
                yown[...] = share

            @pl.when((b != t) | (core != cc))
            def _():
                ysend[h, cc] = share.astype(BF16)
                y_copy(h, cc).start()

        images[...] += lax.dot_general(
            kv2[b], w_all[h], (((1,), (1,)), ((), ())), preferred_element_type=F32
        )
        return carry

    lax.fori_loop(0, KVH, y_loop, 0)

    vg_copy = link(vg_send, vg_recv, VG, partner)

    def half_of_images(first):
        low, high = images[:, :HD], images[:, HD:]
        return jnp.where(first == 0, low, high)

    vg_send[...] = half_of_images(other).astype(BF16)
    vg_copy.start()

    fwd.sent()
    bwd.sent(to_x=(1, 2))
    for k in range(NZ):
        xz_copy(k).wait_send()
    for h in range(KVH):
        fwd.ac_copy(core, h).wait_send()
        core_copy(h).wait_send()
    vision_copy.wait_send()
    for k in near_w:
        w_copy(k).wait_send()

    @pl.when(kind_here != core)
    def _():
        w_copy(0).wait_send()

    for hop in (2, 6):
        @pl.when(lax.div(lax.rem(t + hop, NY), KVH) == core)
        def _():
            for cc in range(2):
                w_third(hop, cc).wait_send()
                w_fourth(hop, cc).wait_send()

    vg_copy.wait_recv()
    vg_ref[0] = (half_of_images(core) + vg_recv[...].astype(F32)).astype(BF16)

    @pl.when(kind_here != core)
    def _():
        link(ysend.at[0, 0], yrecv.at[0], YS, partner).wait_recv()
        yown[...] = yrecv[0].astype(F32)

    grad = yown[...]
    for k in near_first(NY):
        link(ysend.at[0, 0], yrecv.at[k], YS + k, partner).wait_recv()
        grad = grad + yrecv[k].astype(F32)
    wg_ref[...] = grad
    vg_copy.wait_send()
    for h in range(KVH):
        for cc in range(2):
            @pl.when((core * KVH + h != t) | (core != cc))
            def _():
                y_copy(h, cc).wait_send()


def write(*refs):
    sources, targets, sem = refs[:3], refs[3:6], refs[6]
    copies = [
        pltpu.make_async_copy(src, dst, sem.at[n])
        for n, (src, dst) in enumerate(zip(sources, targets))
    ]
    for copy in copies:
        copy.start()
    for copy in copies:
        copy.wait()


def local(queries, out_grad, vision, w_kv, links, img_count):
    rows, width = queries.shape
    hbm = pl.BlockSpec(memory_space=pltpu.HBM)
    vmem = pl.BlockSpec(memory_space=pltpu.VMEM)
    sums = [
        pltpu.VMEM((NX, TOK, HD), BF16),
        pltpu.VMEM((NX, TOK, HD), BF16),
        pltpu.VMEM((TOK, HD), F32),
        pltpu.VMEM((TOK, HD), BF16),
        pltpu.VMEM((NZ, PIECE, HD), BF16),
        pltpu.VMEM((2 * KVH, TOK, HD), BF16),
    ]
    link_slots = jnp.swapaxes(links, 1, 2)
    out_shape = (
        pltpu.VMEM(queries.shape, BF16),
        pltpu.VMEM(vision.shape, BF16),
        pltpu.VMEM(w_kv.shape, F32),
    )
    results = pl.pallas_call(
        body,
        out_shape=out_shape,
        in_specs=[hbm] * 6,
        out_specs=(vmem, vmem, vmem),
        scratch_shapes=[
            pltpu.VMEM((rows, width), BF16),
            pltpu.VMEM((rows, width), BF16),
            pltpu.VMEM((2, TOK, HD), BF16),
            pltpu.VMEM(link_slots.shape, jnp.int32),
            pltpu.VMEM((1, 1), jnp.int32),
            pltpu.VMEM((TOK, HD), F32),
            pltpu.VMEM((2 * HD, TOK), BF16),
            pltpu.VMEM((KVH, 2 * HD, HD), BF16),
            pltpu.VMEM((TOK, HD), BF16),
            pltpu.VMEM((TOK, HD), BF16),
            pltpu.VMEM((KVH, TOK, GROUP * HD), BF16),
            pltpu.VMEM((KVH, 2, TOK, HD), F32),
            pltpu.VMEM((TOK, 2 * HD), F32),
            *sums,
            pltpu.VMEM((KVH, TOK, HD), BF16),
            pltpu.VMEM((KVH, TOK, HD), BF16),
            *sums,
            pltpu.VMEM((NZ, PIECE, HD), BF16),
            pltpu.VMEM((KVH, 2, HD, HD), BF16),
            pltpu.VMEM((NY, HD, HD), BF16),
            pltpu.VMEM((HD, HD), F32),
            pltpu.SemaphoreType.DMA((SEMS,)),
            pltpu.SemaphoreType.DMA((SEMS,)),
            pltpu.SemaphoreType.DMA((6,)),
        ],
        compiler_params=pltpu.CompilerParams(
            collective_id=0, has_side_effects=True, vmem_limit_bytes=40 * 1024 * 1024
        ),
    )(*[
        pltpu.with_memory_space_constraint(a, pltpu.HBM)
        for a in (queries, out_grad, vision, w_kv, link_slots)
    ], img_count.reshape(1, 1))
    return pl.pallas_call(
        write,
        out_shape=tuple(jax.ShapeDtypeStruct(r.shape, r.dtype) for r in results),
        in_specs=[vmem] * 3,
        out_specs=(hbm,) * 3,
        scratch_shapes=[pltpu.SemaphoreType.DMA((3,))],
        compiler_params=pltpu.CompilerParams(vmem_limit_bytes=4 * 1024 * 1024),
    )(*[pltpu.with_memory_space_constraint(a, pltpu.VMEM) for a in results])


def solution(mesh):
    in_specs = (
        P(("txt", "vis"), None),
        P(("txt", "vis"), None),
        P("txt", None, "vis"),
        P("vis", "txt"),
        P("txt", None, None),
        P("txt"),
    )
    out_specs = (P(("txt", "vis"), None), P("txt", None, "vis"), P("vis", "txt"))
    return jax.shard_map(local, mesh=mesh, in_specs=in_specs, out_specs=out_specs, check_vma=False)
```

```python
import jax
import jax.numpy as jnp
from jax import lax
from jax.experimental import pallas as pl
from jax.experimental.pallas import tpu as pltpu
from jax.sharding import PartitionSpec as P

HD = 128
QH = 32
KVH = 4
GROUP = QH // KVH
IMG_DOC = 16
IMG_LEN = 24
TOK = IMG_DOC * IMG_LEN
NZ, NX, NY = 8, 4, 8
PIECE = TOK // NZ
SCALE = HD ** (-0.5)
LOG2E = 1.4426950408889634
MESH = pl.DeviceIdType.MESH
F32, BF16 = jnp.float32, jnp.bfloat16

CORE, XS, ZS, AZ, AX, AC, XZ, OZ = 0, 4, 8, 16, 24, 30, 34, 42
FWD, BWD, WG, YS, VS, VG = 0, 50, 100, 118, 126, 127
SEMS = 128


def near_first(n):
    return sorted(range(1, n), key=lambda k: min(k, n - k))


def far_first(n):
    return near_first(n)[::-1]


def body(
    q_hbm, do_hbm, vision_hbm, w_hbm, links_hbm, count_hbm,
    dq_ref, vg_ref, wg_ref,
    q_ref, do_ref, vision_ref, links_ref, count_ref, bias_ref, vt_ref, w_all, vg_send, vg_recv,
    sg_ref, grads, images,
    xsend1, xrecv1, xown1, zsend1, zrecv1, kv1,
    csend, crecv, xsend2, xrecv2, xown2, zsend2, zrecv2, kv2,
    xz_recv, oz_recv, ysend, yrecv, yown,
    ssem, rsem, lsem,
):
    v = lax.axis_index("vis")
    t = lax.axis_index("txt")
    core = lax.rem(v, 2)
    x = lax.rem(lax.div(v, 2), NX)
    z = lax.div(v, 2 * NX)
    other = 1 - core
    mine = core * KVH + x

    def vis_at(zz, xx, cc):
        return (zz * NX + xx) * 2 + cc

    partner = (vis_at(z, x, other), t)

    def x_dev(k):
        return (vis_at(z, lax.rem(x + k, NX), core), t)

    def z_dev(k):
        return (vis_at(lax.rem(z + k, NZ), x, core), t)

    def xz_dev(i, k):
        return (vis_at(lax.rem(z + k, NZ), lax.rem(x + i, NX), core), t)

    def oz_dev(k):
        return (vis_at(lax.rem(z + k, NZ), x, other), t)

    def y_dev(k, cc=core):
        return (vis_at(z, x, cc), lax.rem(t + k, NY))

    def piece(zz):
        return pl.ds(pl.multiple_of(zz * PIECE, PIECE), PIECE)

    def link(src, dst, sem, dev, arrival=None):
        return pltpu.make_async_remote_copy(
            src_ref=src, dst_ref=dst, send_sem=ssem.at[sem],
            recv_sem=rsem.at[sem if arrival is None else arrival],
            device_id=dev, device_id_type=MESH,
        )

    fetches = [
        pltpu.make_async_copy(src, dst, lsem.at[n])
        for n, (src, dst) in enumerate([
            (vision_hbm.at[0], vision_ref.at[core]), (links_hbm, links_ref),
            (count_hbm, count_ref), (q_hbm, q_ref), (do_hbm, do_ref),
        ])
    ]
    for fetch in fetches:
        fetch.start()

    barrier = pltpu.get_barrier_semaphore()
    partners = (
        [y_dev(k, cc) for k in far_first(NY) for cc in (core, other)]
        + [z_dev(k) for k in far_first(NZ)]
        + [x_dev(k) for k in far_first(NX)]
        + [partner]
        + [xz_dev(1, k) for k in range(1, NZ)]
        + [oz_dev(k) for k in range(1, NZ)]
    )
    for dev in partners:
        pl.semaphore_signal(barrier, inc=1, device_id=dev, device_id_type=MESH)
    pl.semaphore_wait(barrier, len(partners))

    kind_here = lax.div(t, KVH)

    def w_slot(b, cc, low=0, size=HD):
        rows = pl.ds(pl.multiple_of(cc * HD + low, HD // 2), size)
        return w_all.at[lax.rem(b, KVH), rows, :]

    def w_copy(k):
        place = WG + (NY - k if k else 0) * 2
        return link(w_hbm, w_slot(t, core), place + core, y_dev(k, kind_here), place + core)

    def w_third(j, cc):
        slot = w_slot(lax.rem(t + j, NY), cc)
        up = j == 2
        return link(slot, slot, WG + (3 if up else 5) * 2 + cc, y_dev(NY - 1 if up else 1))

    def w_fourth(j, cc):
        up = j == 2
        slot = w_slot(lax.rem(t + j, NY), cc, 0 if up else HD // 2, HD // 2)
        return link(slot, slot, WG + (4 if up else 8) * 2 + cc, y_dev(NY - 2 if up else 2))

    vision_copy = link(vision_hbm.at[0], vision_ref.at[core], VS, partner)
    w_here = pltpu.make_async_copy(w_hbm, w_slot(t, core), lsem.at[5])
    near_w = (1, NY - 1, 2, NY - 2)

    for k in near_w:
        w_copy(k).start()

    @pl.when(kind_here == core)
    def _():
        w_here.start()

    @pl.when(kind_here != core)
    def _():
        w_copy(0).start()

    vision_copy.start()
    for fetch in fetches[:3]:
        fetch.wait()

    block = lax.broadcasted_iota(jnp.int32, links_ref.shape[1:], 1)
    slot = lax.broadcasted_iota(jnp.int32, (IMG_DOC, 1), 0)
    linked = jnp.sum(jnp.where(block == v, links_ref[0], 0), axis=1, keepdims=True)
    bias = jnp.where((linked == 1) & (slot < count_ref[...]), 0.0, -1e30)
    for s in range(IMG_DOC):
        bias_ref[s * IMG_LEN : (s + 1) * IMG_LEN, :] = jnp.broadcast_to(
            bias[s : s + 1, :], (IMG_LEN, HD)
        )

    class Sums:
        def __init__(self, base, xsend, xrecv, xown, zsend, zrecv, kv):
            self.base = base
            self.xsend, self.xrecv, self.xown = xsend, xrecv, xown
            self.zsend, self.zrecv, self.kv = zsend, zrecv, kv

        def x_copy(self, k):
            return link(self.xsend.at[k], self.xrecv.at[k], self.base + XS + k, x_dev(k))

        def z_copy(self, k):
            rows = piece(lax.rem(z + k, NZ))
            return link(self.zsend.at[rows, :], self.zrecv.at[k], self.base + ZS + k, z_dev(k))

        def az_copy(self, k, zz):
            ref = self.kv.at[mine, piece(zz), :]
            return link(ref, ref, self.base + AZ + k, z_dev(k))

        def half_block(self, h, part):
            return self.kv.at[core * KVH + h, pl.ds(part * (TOK // 2), TOK // 2), :]

        def ax_copy(self, k, h, part):
            half = self.half_block(h, part)
            return link(half, half, self.base + AX + (k - 1) + part, x_dev(k))

        def across(self, i):
            part = 0 if i == 1 else 1
            half = self.half_block(lax.rem(x + i, NX), part)
            return link(half, half, self.base + AX + 4 + part, x_dev(NX - i))

        def ac_copy(self, kind, h):
            ref = self.kv.at[kind * KVH + h]
            return link(ref, ref, self.base + AC + h, partner)

        def x_step(self, h, total):
            k = lax.rem(h - x + NX, NX)

            @pl.when(k == 0)
            def _():
                self.xown[...] = total

            @pl.when(k != 0)
            def _():
                self.xsend[k] = total.astype(BF16)
                self.x_copy(k).start()

        def z_stage(self, first=lambda: None, share=False, from_x=(1, 3, 2), more=lambda part: part):
            total = self.xown[...]
            for k in from_x:
                self.x_copy(k).wait_recv()
                total = total + self.xrecv[k].astype(F32)
            self.xown[...] = total
            self.zsend[...] = total.astype(BF16)
            for k in far_first(NZ):
                self.z_copy(k).start()
            first()
            part = self.xown[piece(z), :]
            for k in near_first(NZ):
                self.z_copy(k).wait_recv()
                part = part + self.zrecv[k].astype(F32)
            self.kv[mine, piece(z), :] = more(part).astype(BF16)
            for k in far_first(NZ):
                self.az_copy(k, z).start()
            for k in near_first(NZ):
                self.az_copy(k, lax.rem(z - k + NZ, NZ)).wait_recv()
            if share:
                self.ac_copy(core, x).start()
            for k, half in ((3, 0), (1, 1), (3, 1), (1, 0)):
                self.ax_copy(k, x, half).start()

        def pass_on(self, i):
            h = lax.rem(x + i, NX)
            self.ax_copy(NX - i, h, 0 if i == 1 else 1).wait_recv()
            self.across(i).start()

        def x_arrive(self, i, share=False):
            h = lax.rem(x + i, NX)
            if i == 2:
                for part in range(2):
                    half = self.half_block(h, part)
                    link(half, half, self.base + AX + 4 + part, x_dev(1)).wait_recv()
            else:
                self.ax_copy(NX - i, h, 1 if i == 1 else 0).wait_recv()
            if share:
                self.ac_copy(core, h).start()

        def partner_arrive(self, i):
            self.ac_copy(other, lax.rem(x + i, NX)).wait_recv()

        def sent(self, to_x=(1, 2, 3)):
            for k in to_x:
                self.x_copy(k).wait_send()
            for k in (1, 3):
                for part in range(2):
                    self.ax_copy(k, x, part).wait_send()
                self.across(k).wait_send()
            for k in range(1, NZ):
                self.z_copy(k).wait_send()
                self.az_copy(k, z).wait_send()

    fwd = Sums(FWD, xsend1, xrecv1, xown1, zsend1, zrecv1, kv1)
    bwd = Sums(BWD, xsend2, xrecv2, xown2, zsend2, zrecv2, kv2)

    def near(n):
        far = lax.div(n + 1, 2)
        return jnp.where(lax.rem(n, 2) == 1, far, lax.rem(NY - far, NY))

    vision_copy.wait_recv()
    vt_ref[:HD, :] = vision_ref[0].T
    vt_ref[HD:, :] = vision_ref[1].T

    def w_loop(n, carry):
        j = near(n)
        b = lax.rem(t + j, NY)
        h = lax.rem(b, KVH)

        @pl.when(lax.div(b, KVH) == core)
        def _():
            @pl.when(j == 0)
            def _():
                w_here.wait()
                link(w_hbm, w_slot(b, other), WG + other, partner).wait_recv()

            for cc in range(2):
                @pl.when((j != 0) & (j != 4))
                def _():
                    link(w_hbm, w_slot(b, cc), WG + j * 2 + cc, partner).wait_recv()

                for hop in (2, 6):
                    @pl.when(j == hop)
                    def _():
                        w_third(hop, cc).start()
                        w_fourth(hop, cc).start()

                @pl.when(j == 4)
                def _():
                    for place, low in ((4, 0), (8, HD // 2)):
                        half = w_slot(b, cc, low, HD // 2)
                        link(half, half, WG + place * 2 + cc, partner).wait_recv()

            images = jnp.concatenate([vision_ref[0], vision_ref[1]], axis=1)
            part = jnp.dot(images, w_all[h], preferred_element_type=F32)
            fwd.x_step(h, part)

        return carry

    lax.fori_loop(0, NY, w_loop, 0)
    fwd.z_stage(share=True)

    for fetch in fetches[3:]:
        fetch.wait()

    def core_copy(h):
        return link(csend.at[h], crecv.at[h], BWD + CORE + h, partner)

    def xz_copy(k):
        rows = piece(lax.rem(z + k, NZ))
        return link(xsend2.at[3, rows, :], xz_recv.at[k], BWD + XZ + k, xz_dev(3, k))

    def last_step():
        h = lax.rem(x + 3, NX)
        core_copy(h).wait_recv()
        xsend2[3] = (grads[h, core] + crecv[h].astype(F32)).astype(BF16)
        for k in [*far_first(NZ), 0]:
            xz_copy(k).start()

    def oz_copy(k):
        rows = piece(lax.rem(z + k, NZ))
        return link(csend.at[x, rows, :], oz_recv.at[k], BWD + OZ + k, oz_dev(k))

    def last_arrive(part):
        for k in [0, *near_first(NZ)]:
            oz_copy(k).wait_recv()
            part = part + oz_recv[k].astype(F32)
        for k in [0, *near_first(NZ)]:
            xz_copy(k).wait_recv()
            part = part + xz_recv[k].astype(F32)
        return part

    def head_step(h):
        core_copy(h).wait_recv()
        bwd.x_step(h, grads[h, core] + crecv[h].astype(F32))

    HALF = GROUP // 2

    def attend(u, carry):
        mine_now = (u == 0) | (u == 2 * KVH - 1)
        i = jnp.where(mine_now, 0, lax.div(u + 1, 2))
        half = jnp.where(mine_now, lax.div(u, 2 * KVH - 1), lax.rem(u + 1, 2))
        h = lax.rem(x + i, NX)
        base = h * GROUP * HD + half * HALF * HD

        def columns(j):
            return pl.ds(pl.multiple_of(base + j * HD, HD), HD)

        @pl.when(u == 1)
        def _():
            fwd.pass_on(1)
            fwd.pass_on(3)
            fwd.x_arrive(1, share=True)
            fwd.x_arrive(3, share=True)

        @pl.when(u == 2)
        def _():
            fwd.x_arrive(2, share=True)

        @pl.when(half == 0)
        def _():
            fwd.partner_arrive(i)

        dims = (((1,), (1,)), ((), ()))
        bias = jnp.concatenate([bias_ref[...]] * 2, axis=1)
        key_part = value_part = None
        for j in range(0, HALF, 2):
            q = jnp.concatenate([q_ref[:, columns(j)], q_ref[:, columns(j + 1)]], axis=0)
            do = jnp.concatenate([do_ref[:, columns(j)], do_ref[:, columns(j + 1)]], axis=0)
            s = lax.dot_general(kv1[h], q, dims, preferred_element_type=F32)
            g = lax.dot_general(kv1[KVH + h], do, dims, preferred_element_type=F32)
            s = s * (SCALE * LOG2E) + bias
            e = jnp.exp2(s - jnp.max(s, axis=0, keepdims=True))
            norm = 1.0 / jnp.sum(e, axis=0, keepdims=True)
            delta = jnp.sum(e * g, axis=0, keepdims=True) * norm
            probs = e * norm
            score_grad = (probs * (g - delta)).astype(BF16)
            place = pl.ds(pl.multiple_of((half * HALF + j) * HD, HD), 2 * HD)
            sg_ref[h, :, place] = score_grad
            key_more = jnp.dot(score_grad, q, preferred_element_type=F32)
            value_more = jnp.dot(probs.astype(BF16), do, preferred_element_type=F32)
            key_part = key_more if j == 0 else key_part + key_more
            value_part = value_more if j == 0 else value_part + value_more
        key_part = key_part * SCALE

        @pl.when(half == 0)
        def _():
            grads[h, 0] = key_part
            grads[h, 1] = value_part

        @pl.when(half == 1)
        def _():
            grads[h, 0] += key_part
            grads[h, 1] += value_part
            csend[h] = grads[h, other].astype(BF16)

            @pl.when(u < 2 * KVH - 1)
            def _():
                core_copy(h).start()

        for when, done in ((3, 1), (5, 2)):
            @pl.when(u == when)
            def _():
                head_step(lax.rem(x + done, NX))

        return carry

    lax.fori_loop(0, 2 * KVH, attend, 0)
    last_step()

    def query_grads(low, high):
        def one(i, carry):
            h = lax.rem(x + i, NX)
            dq = jnp.dot(kv1[h].T, sg_ref[h], preferred_element_type=F32) * SCALE
            for j in range(GROUP):
                place = pl.ds(pl.multiple_of((h * GROUP + j) * HD, HD), HD)
                dq_ref[:, place] = dq[:, j * HD : (j + 1) * HD].T.astype(BF16)
            return carry

        lax.fori_loop(low, high, one, 0)

    for k in [*far_first(NZ), 0]:
        oz_copy(k).start()
    bwd.x_step(x, grads[x, core])
    bwd.z_stage(lambda: query_grads(0, KVH), from_x=(1, 2), more=last_arrive)

    def y_copy(h, cc):
        k = lax.rem(core * KVH + h - t + NY, NY)
        return link(ysend.at[h, cc], yrecv.at[k], YS + h * 2 + cc, y_dev(k, cc), YS + k)

    images[...] = jnp.zeros((TOK, 2 * HD), F32)

    def y_loop(n, carry):
        i = jnp.where(n < 2, n, 5 - n)
        h = lax.rem(x + i, NX)
        b = core * KVH + h

        @pl.when(n == 1)
        def _():
            bwd.pass_on(1)
            bwd.pass_on(3)

        for when, place in ((1, 1), (2, 3), (3, 2)):
            @pl.when(n == when)
            def _():
                bwd.x_arrive(place)

        part = jnp.dot(vt_ref[...], kv2[b], preferred_element_type=F32)
        for cc in range(2):
            share = part[cc * HD : (cc + 1) * HD, :]

            @pl.when((b == t) & (core == cc))
            def _():
                yown[...] = share

            @pl.when((b != t) | (core != cc))
            def _():
                ysend[h, cc] = share.astype(BF16)
                y_copy(h, cc).start()

        return carry

    lax.fori_loop(0, KVH, y_loop, 0)

    def image_loop(h, carry):
        images[...] += lax.dot_general(
            kv2[core * KVH + h], w_all[h], (((1,), (1,)), ((), ())), preferred_element_type=F32
        )
        return carry

    lax.fori_loop(0, KVH, image_loop, 0)

    vg_copy = link(vg_send, vg_recv, VG, partner)

    def half_of_images(first):
        low, high = images[:, :HD], images[:, HD:]
        return jnp.where(first == 0, low, high)

    vg_send[...] = half_of_images(other).astype(BF16)
    vg_copy.start()

    fwd.sent()
    bwd.sent(to_x=(1, 2))
    for k in range(NZ):
        xz_copy(k).wait_send()
        oz_copy(k).wait_send()
    for h in range(KVH):
        fwd.ac_copy(core, h).wait_send()
    for i in range(1, KVH):
        core_copy(lax.rem(x + i, NX)).wait_send()
    vision_copy.wait_send()
    for k in near_w:
        w_copy(k).wait_send()

    @pl.when(kind_here != core)
    def _():
        w_copy(0).wait_send()

    for hop in (2, 6):
        @pl.when(lax.div(lax.rem(t + hop, NY), KVH) == core)
        def _():
            for cc in range(2):
                w_third(hop, cc).wait_send()
                w_fourth(hop, cc).wait_send()

    vg_copy.wait_recv()
    vg_ref[0] = (half_of_images(core) + vg_recv[...].astype(F32)).astype(BF16)

    @pl.when(kind_here != core)
    def _():
        link(ysend.at[0, 0], yrecv.at[0], YS, partner).wait_recv()
        yown[...] = yrecv[0].astype(F32)

    grad = yown[...]
    for k in near_first(NY):
        link(ysend.at[0, 0], yrecv.at[k], YS + k, partner).wait_recv()
        grad = grad + yrecv[k].astype(F32)
    wg_ref[...] = grad
    vg_copy.wait_send()
    for h in range(KVH):
        for cc in range(2):
            @pl.when((core * KVH + h != t) | (core != cc))
            def _():
                y_copy(h, cc).wait_send()


def write(*refs):
    sources, targets, sem = refs[:3], refs[3:6], refs[6]
    copies = [
        pltpu.make_async_copy(src, dst, sem.at[n])
        for n, (src, dst) in enumerate(zip(sources, targets))
    ]
    for copy in copies:
        copy.start()
    for copy in copies:
        copy.wait()


def local(queries, out_grad, vision, w_kv, links, img_count):
    rows, width = queries.shape
    hbm = pl.BlockSpec(memory_space=pltpu.HBM)
    vmem = pl.BlockSpec(memory_space=pltpu.VMEM)
    sums = [
        pltpu.VMEM((NX, TOK, HD), BF16),
        pltpu.VMEM((NX, TOK, HD), BF16),
        pltpu.VMEM((TOK, HD), F32),
        pltpu.VMEM((TOK, HD), BF16),
        pltpu.VMEM((NZ, PIECE, HD), BF16),
        pltpu.VMEM((2 * KVH, TOK, HD), BF16),
    ]
    link_slots = jnp.swapaxes(links, 1, 2)
    out_shape = (
        pltpu.VMEM(queries.shape, BF16),
        pltpu.VMEM(vision.shape, BF16),
        pltpu.VMEM(w_kv.shape, F32),
    )
    results = pl.pallas_call(
        body,
        out_shape=out_shape,
        in_specs=[hbm] * 6,
        out_specs=(vmem, vmem, vmem),
        scratch_shapes=[
            pltpu.VMEM((rows, width), BF16),
            pltpu.VMEM((rows, width), BF16),
            pltpu.VMEM((2, TOK, HD), BF16),
            pltpu.VMEM(link_slots.shape, jnp.int32),
            pltpu.VMEM((1, 1), jnp.int32),
            pltpu.VMEM((TOK, HD), F32),
            pltpu.VMEM((2 * HD, TOK), BF16),
            pltpu.VMEM((KVH, 2 * HD, HD), BF16),
            pltpu.VMEM((TOK, HD), BF16),
            pltpu.VMEM((TOK, HD), BF16),
            pltpu.VMEM((KVH, TOK, GROUP * HD), BF16),
            pltpu.VMEM((KVH, 2, TOK, HD), F32),
            pltpu.VMEM((TOK, 2 * HD), F32),
            *sums,
            pltpu.VMEM((KVH, TOK, HD), BF16),
            pltpu.VMEM((KVH, TOK, HD), BF16),
            *sums,
            pltpu.VMEM((NZ, PIECE, HD), BF16),
            pltpu.VMEM((NZ, PIECE, HD), BF16),
            pltpu.VMEM((KVH, 2, HD, HD), BF16),
            pltpu.VMEM((NY, HD, HD), BF16),
            pltpu.VMEM((HD, HD), F32),
            pltpu.SemaphoreType.DMA((SEMS,)),
            pltpu.SemaphoreType.DMA((SEMS,)),
            pltpu.SemaphoreType.DMA((6,)),
        ],
        compiler_params=pltpu.CompilerParams(
            collective_id=0, has_side_effects=True, vmem_limit_bytes=40 * 1024 * 1024
        ),
    )(*[
        pltpu.with_memory_space_constraint(a, pltpu.HBM)
        for a in (queries, out_grad, vision, w_kv, link_slots)
    ], img_count.reshape(1, 1))
    return pl.pallas_call(
        write,
        out_shape=tuple(jax.ShapeDtypeStruct(r.shape, r.dtype) for r in results),
        in_specs=[vmem] * 3,
        out_specs=(hbm,) * 3,
        scratch_shapes=[pltpu.SemaphoreType.DMA((3,))],
        compiler_params=pltpu.CompilerParams(vmem_limit_bytes=4 * 1024 * 1024),
    )(*[pltpu.with_memory_space_constraint(a, pltpu.VMEM) for a in results])


def solution(mesh):
    in_specs = (
        P(("txt", "vis"), None),
        P(("txt", "vis"), None),
        P("txt", None, "vis"),
        P("vis", "txt"),
        P("txt", None, None),
        P("txt"),
    )
    out_specs = (P(("txt", "vis"), None), P("txt", None, "vis"), P("vis", "txt"))
    return jax.shard_map(local, mesh=mesh, in_specs=in_specs, out_specs=out_specs, check_vma=False)
```

```python
import jax
import jax.numpy as jnp
from jax import lax
from jax.experimental import pallas as pl
from jax.experimental.pallas import tpu as pltpu
from jax.sharding import PartitionSpec as P

HD = 128
QH = 32
KVH = 4
GROUP = QH // KVH
IMG_DOC = 16
IMG_LEN = 24
TOK = IMG_DOC * IMG_LEN
NZ, NX, NY = 8, 4, 8
PIECE = TOK // NZ
SCALE = HD ** (-0.5)
LOG2E = 1.4426950408889634
MESH = pl.DeviceIdType.MESH
F32, BF16 = jnp.float32, jnp.bfloat16

CORE, XS, ZS, AZ, AX, AC, XZ = 0, 4, 8, 16, 24, 30, 34
FWD, BWD, WG, YS, VS, VG = 0, 42, 84, 102, 110, 111
SEMS = 112


def near_first(n):
    return sorted(range(1, n), key=lambda k: min(k, n - k))


def far_first(n):
    return near_first(n)[::-1]


def body(
    q_hbm, do_hbm, vision_hbm, w_hbm, links_hbm, count_hbm,
    dq_ref, vg_ref, wg_ref,
    q_ref, do_ref, vision_ref, links_ref, count_ref, bias_ref, vt_ref, w_all, vg_send, vg_recv,
    sg_ref, grads, images,
    xsend1, xrecv1, xown1, zsend1, zrecv1, kv1,
    csend, crecv, xsend2, xrecv2, xown2, zsend2, zrecv2, kv2,
    xz_recv, ysend, yrecv, yown,
    ssem, rsem, lsem,
):
    v = lax.axis_index("vis")
    t = lax.axis_index("txt")
    core = lax.rem(v, 2)
    x = lax.rem(lax.div(v, 2), NX)
    z = lax.div(v, 2 * NX)
    other = 1 - core
    mine = core * KVH + x

    def vis_at(zz, xx, cc):
        return (zz * NX + xx) * 2 + cc

    partner = (vis_at(z, x, other), t)

    def x_dev(k):
        return (vis_at(z, lax.rem(x + k, NX), core), t)

    def z_dev(k):
        return (vis_at(lax.rem(z + k, NZ), x, core), t)

    def xz_dev(i, k):
        return (vis_at(lax.rem(z + k, NZ), lax.rem(x + i, NX), core), t)

    def y_dev(k, cc=core):
        return (vis_at(z, x, cc), lax.rem(t + k, NY))

    def piece(zz):
        return pl.ds(pl.multiple_of(zz * PIECE, PIECE), PIECE)

    def link(src, dst, sem, dev, arrival=None):
        return pltpu.make_async_remote_copy(
            src_ref=src, dst_ref=dst, send_sem=ssem.at[sem],
            recv_sem=rsem.at[sem if arrival is None else arrival],
            device_id=dev, device_id_type=MESH,
        )

    fetches = [
        pltpu.make_async_copy(src, dst, lsem.at[n])
        for n, (src, dst) in enumerate([
            (vision_hbm.at[0], vision_ref.at[core]), (links_hbm, links_ref),
            (count_hbm, count_ref), (q_hbm, q_ref), (do_hbm, do_ref),
        ])
    ]
    for fetch in fetches:
        fetch.start()

    barrier = pltpu.get_barrier_semaphore()
    partners = (
        [y_dev(k, cc) for k in far_first(NY) for cc in (core, other)]
        + [z_dev(k) for k in far_first(NZ)]
        + [x_dev(k) for k in far_first(NX)]
        + [partner]
        + [xz_dev(1, k) for k in range(1, NZ)]
    )
    for dev in partners:
        pl.semaphore_signal(barrier, inc=1, device_id=dev, device_id_type=MESH)
    pl.semaphore_wait(barrier, len(partners))

    kind_here = lax.div(t, KVH)

    def w_slot(b, cc, low=0, size=HD):
        rows = pl.ds(pl.multiple_of(cc * HD + low, HD // 2), size)
        return w_all.at[lax.rem(b, KVH), rows, :]

    def w_copy(k):
        place = WG + (NY - k if k else 0) * 2
        return link(w_hbm, w_slot(t, core), place + core, y_dev(k, kind_here), place + core)

    def w_third(j, cc):
        slot = w_slot(lax.rem(t + j, NY), cc)
        up = j == 2
        return link(slot, slot, WG + (3 if up else 5) * 2 + cc, y_dev(NY - 1 if up else 1))

    def w_fourth(j, cc):
        up = j == 2
        slot = w_slot(lax.rem(t + j, NY), cc, 0 if up else HD // 2, HD // 2)
        return link(slot, slot, WG + (4 if up else 8) * 2 + cc, y_dev(NY - 2 if up else 2))

    vision_copy = link(vision_hbm.at[0], vision_ref.at[core], VS, partner)
    w_here = pltpu.make_async_copy(w_hbm, w_slot(t, core), lsem.at[5])
    near_w = (1, NY - 1, 2, NY - 2)

    for k in near_w:
        w_copy(k).start()

    @pl.when(kind_here == core)
    def _():
        w_here.start()

    @pl.when(kind_here != core)
    def _():
        w_copy(0).start()

    vision_copy.start()
    for fetch in fetches[:3]:
        fetch.wait()

    block = lax.broadcasted_iota(jnp.int32, links_ref.shape[1:], 1)
    slot = lax.broadcasted_iota(jnp.int32, (IMG_DOC, 1), 0)
    linked = jnp.sum(jnp.where(block == v, links_ref[0], 0), axis=1, keepdims=True)
    bias = jnp.where((linked == 1) & (slot < count_ref[...]), 0.0, -1e30)
    for s in range(IMG_DOC):
        bias_ref[s * IMG_LEN : (s + 1) * IMG_LEN, :] = jnp.broadcast_to(
            bias[s : s + 1, :], (IMG_LEN, HD)
        )

    class Sums:
        def __init__(self, base, xsend, xrecv, xown, zsend, zrecv, kv):
            self.base = base
            self.xsend, self.xrecv, self.xown = xsend, xrecv, xown
            self.zsend, self.zrecv, self.kv = zsend, zrecv, kv

        def x_copy(self, k):
            return link(self.xsend.at[k], self.xrecv.at[k], self.base + XS + k, x_dev(k))

        def z_copy(self, k):
            rows = piece(lax.rem(z + k, NZ))
            return link(self.zsend.at[rows, :], self.zrecv.at[k], self.base + ZS + k, z_dev(k))

        def az_copy(self, k, zz):
            ref = self.kv.at[mine, piece(zz), :]
            return link(ref, ref, self.base + AZ + k, z_dev(k))

        def half_block(self, h, part):
            return self.kv.at[core * KVH + h, pl.ds(part * (TOK // 2), TOK // 2), :]

        def ax_copy(self, k, h, part):
            half = self.half_block(h, part)
            return link(half, half, self.base + AX + (k - 1) + part, x_dev(k))

        def across(self, i):
            part = 0 if i == 1 else 1
            half = self.half_block(lax.rem(x + i, NX), part)
            return link(half, half, self.base + AX + 4 + part, x_dev(NX - i))

        def ac_copy(self, kind, h):
            ref = self.kv.at[kind * KVH + h]
            return link(ref, ref, self.base + AC + h, partner)

        def x_step(self, h, total):
            k = lax.rem(h - x + NX, NX)

            @pl.when(k == 0)
            def _():
                self.xown[...] = total

            @pl.when(k != 0)
            def _():
                self.xsend[k] = total.astype(BF16)
                self.x_copy(k).start()

        def z_stage(self, first=lambda: None, share=False, from_x=(1, 3, 2), more=lambda part: part):
            total = self.xown[...]
            for k in from_x:
                self.x_copy(k).wait_recv()
                total = total + self.xrecv[k].astype(F32)
            self.xown[...] = total
            self.zsend[...] = total.astype(BF16)
            for k in far_first(NZ):
                self.z_copy(k).start()
            first()
            part = self.xown[piece(z), :]
            for k in near_first(NZ):
                self.z_copy(k).wait_recv()
                part = part + self.zrecv[k].astype(F32)
            self.kv[mine, piece(z), :] = more(part).astype(BF16)
            for k in far_first(NZ):
                self.az_copy(k, z).start()
            for k in near_first(NZ):
                self.az_copy(k, lax.rem(z - k + NZ, NZ)).wait_recv()
            if share:
                self.ac_copy(core, x).start()
            for k, half in ((3, 0), (1, 1), (3, 1), (1, 0)):
                self.ax_copy(k, x, half).start()

        def pass_on(self, i):
            h = lax.rem(x + i, NX)
            self.ax_copy(NX - i, h, 0 if i == 1 else 1).wait_recv()
            self.across(i).start()

        def x_arrive(self, i, share=False):
            h = lax.rem(x + i, NX)
            if i == 2:
                for part in range(2):
                    half = self.half_block(h, part)
                    link(half, half, self.base + AX + 4 + part, x_dev(1)).wait_recv()
            else:
                self.ax_copy(NX - i, h, 1 if i == 1 else 0).wait_recv()
            if share:
                self.ac_copy(core, h).start()

        def partner_arrive(self, i):
            self.ac_copy(other, lax.rem(x + i, NX)).wait_recv()

        def sent(self, to_x=(1, 2, 3)):
            for k in to_x:
                self.x_copy(k).wait_send()
            for k in (1, 3):
                for part in range(2):
                    self.ax_copy(k, x, part).wait_send()
                self.across(k).wait_send()
            for k in range(1, NZ):
                self.z_copy(k).wait_send()
                self.az_copy(k, z).wait_send()

    fwd = Sums(FWD, xsend1, xrecv1, xown1, zsend1, zrecv1, kv1)
    bwd = Sums(BWD, xsend2, xrecv2, xown2, zsend2, zrecv2, kv2)

    def near(n):
        far = lax.div(n + 1, 2)
        return jnp.where(lax.rem(n, 2) == 1, far, lax.rem(NY - far, NY))

    vision_copy.wait_recv()
    vt_ref[:HD, :] = vision_ref[0].T
    vt_ref[HD:, :] = vision_ref[1].T

    def w_loop(n, carry):
        j = near(n)
        b = lax.rem(t + j, NY)
        h = lax.rem(b, KVH)

        @pl.when(lax.div(b, KVH) == core)
        def _():
            @pl.when(j == 0)
            def _():
                w_here.wait()
                link(w_hbm, w_slot(b, other), WG + other, partner).wait_recv()

            for cc in range(2):
                @pl.when((j != 0) & (j != 4))
                def _():
                    link(w_hbm, w_slot(b, cc), WG + j * 2 + cc, partner).wait_recv()

                for hop in (2, 6):
                    @pl.when(j == hop)
                    def _():
                        w_third(hop, cc).start()
                        w_fourth(hop, cc).start()

                @pl.when(j == 4)
                def _():
                    for place, low in ((4, 0), (8, HD // 2)):
                        half = w_slot(b, cc, low, HD // 2)
                        link(half, half, WG + place * 2 + cc, partner).wait_recv()

            images = jnp.concatenate([vision_ref[0], vision_ref[1]], axis=1)
            part = jnp.dot(images, w_all[h], preferred_element_type=F32)
            fwd.x_step(h, part)

        return carry

    lax.fori_loop(0, NY, w_loop, 0)
    fwd.z_stage(share=True)

    for fetch in fetches[3:]:
        fetch.wait()

    def core_copy(h):
        return link(csend.at[h], crecv.at[h], BWD + CORE + h, partner)

    def xz_copy(k):
        rows = piece(lax.rem(z + k, NZ))
        return link(xsend2.at[3, rows, :], xz_recv.at[k], BWD + XZ + k, xz_dev(3, k))

    def last_step():
        h = lax.rem(x + 3, NX)
        core_copy(h).wait_recv()
        xsend2[3] = (grads[h, core] + crecv[h].astype(F32)).astype(BF16)
        for k in [*far_first(NZ), 0]:
            xz_copy(k).start()

    def last_arrive(part):
        for k in [0, *near_first(NZ)]:
            xz_copy(k).wait_recv()
            part = part + xz_recv[k].astype(F32)
        return part

    def head_step(h):
        core_copy(h).wait_recv()
        bwd.x_step(h, grads[h, core] + crecv[h].astype(F32))

    HALF = GROUP // 2

    def attend(u, carry):
        mine_now = (u == 0) | (u == 2 * KVH - 1)
        i = jnp.where(mine_now, 0, lax.div(u + 1, 2))
        half = jnp.where(mine_now, lax.div(u, 2 * KVH - 1), lax.rem(u + 1, 2))
        h = lax.rem(x + i, NX)
        base = h * GROUP * HD + half * HALF * HD

        def columns(j):
            return pl.ds(pl.multiple_of(base + j * HD, HD), HD)

        @pl.when(u == 1)
        def _():
            fwd.pass_on(1)
            fwd.pass_on(3)
            fwd.x_arrive(1, share=True)
            fwd.x_arrive(3, share=True)

        @pl.when(u == 2)
        def _():
            fwd.x_arrive(2, share=True)

        @pl.when(half == 0)
        def _():
            fwd.partner_arrive(i)

        dims = (((1,), (1,)), ((), ()))
        bias = jnp.concatenate([bias_ref[...]] * 2, axis=1)
        key_part = value_part = None
        for j in range(0, HALF, 2):
            q = jnp.concatenate([q_ref[:, columns(j)], q_ref[:, columns(j + 1)]], axis=0)
            do = jnp.concatenate([do_ref[:, columns(j)], do_ref[:, columns(j + 1)]], axis=0)
            s = lax.dot_general(kv1[h], q, dims, preferred_element_type=F32)
            g = lax.dot_general(kv1[KVH + h], do, dims, preferred_element_type=F32)
            s = s * (SCALE * LOG2E) + bias
            e = jnp.exp2(s - jnp.max(s, axis=0, keepdims=True))
            norm = 1.0 / jnp.sum(e, axis=0, keepdims=True)
            delta = jnp.sum(e * g, axis=0, keepdims=True) * norm
            probs = e * norm
            score_grad = (probs * (g - delta)).astype(BF16)
            place = pl.ds(pl.multiple_of((half * HALF + j) * HD, HD), 2 * HD)
            sg_ref[h, :, place] = score_grad
            key_more = jnp.dot(score_grad, q, preferred_element_type=F32)
            value_more = jnp.dot(probs.astype(BF16), do, preferred_element_type=F32)
            key_part = key_more if j == 0 else key_part + key_more
            value_part = value_more if j == 0 else value_part + value_more
        key_part = key_part * SCALE

        @pl.when(half == 0)
        def _():
            grads[h, 0] = key_part
            grads[h, 1] = value_part

        @pl.when(half == 1)
        def _():
            grads[h, 0] += key_part
            grads[h, 1] += value_part
            csend[h] = grads[h, other].astype(BF16)
            core_copy(h).start()

        for when, done in ((3, 1), (5, 2)):
            @pl.when(u == when)
            def _():
                head_step(lax.rem(x + done, NX))

        return carry

    lax.fori_loop(0, 2 * KVH, attend, 0)
    last_step()

    def query_grads(low, high):
        def one(i, carry):
            h = lax.rem(x + i, NX)
            dq = jnp.dot(kv1[h].T, sg_ref[h], preferred_element_type=F32) * SCALE
            for j in range(GROUP):
                place = pl.ds(pl.multiple_of((h * GROUP + j) * HD, HD), HD)
                dq_ref[:, place] = dq[:, j * HD : (j + 1) * HD].T.astype(BF16)
            return carry

        lax.fori_loop(low, high, one, 0)

    query_grads(0, 1)
    head_step(x)
    bwd.z_stage(lambda: query_grads(1, KVH), from_x=(1, 2), more=last_arrive)

    def y_copy(h, cc):
        k = lax.rem(core * KVH + h - t + NY, NY)
        return link(ysend.at[h, cc], yrecv.at[k], YS + h * 2 + cc, y_dev(k, cc), YS + k)

    images[...] = jnp.zeros((TOK, 2 * HD), F32)

    def y_loop(n, carry):
        i = jnp.where(n < 2, n, 5 - n)
        h = lax.rem(x + i, NX)
        b = core * KVH + h

        @pl.when(n == 1)
        def _():
            bwd.pass_on(1)
            bwd.pass_on(3)

        for when, place in ((1, 1), (2, 3), (3, 2)):
            @pl.when(n == when)
            def _():
                bwd.x_arrive(place)

        part = jnp.dot(vt_ref[...], kv2[b], preferred_element_type=F32)
        for cc in range(2):
            share = part[cc * HD : (cc + 1) * HD, :]

            @pl.when((b == t) & (core == cc))
            def _():
                yown[...] = share

            @pl.when((b != t) | (core != cc))
            def _():
                ysend[h, cc] = share.astype(BF16)
                y_copy(h, cc).start()

        return carry

    lax.fori_loop(0, KVH, y_loop, 0)

    def image_loop(h, carry):
        images[...] += lax.dot_general(
            kv2[core * KVH + h], w_all[h], (((1,), (1,)), ((), ())), preferred_element_type=F32
        )
        return carry

    lax.fori_loop(0, KVH, image_loop, 0)

    vg_copy = link(vg_send, vg_recv, VG, partner)

    def half_of_images(first):
        low, high = images[:, :HD], images[:, HD:]
        return jnp.where(first == 0, low, high)

    vg_send[...] = half_of_images(other).astype(BF16)
    vg_copy.start()

    fwd.sent()
    bwd.sent(to_x=(1, 2))
    for k in range(NZ):
        xz_copy(k).wait_send()
    for h in range(KVH):
        fwd.ac_copy(core, h).wait_send()
        core_copy(h).wait_send()
    vision_copy.wait_send()
    for k in near_w:
        w_copy(k).wait_send()

    @pl.when(kind_here != core)
    def _():
        w_copy(0).wait_send()

    for hop in (2, 6):
        @pl.when(lax.div(lax.rem(t + hop, NY), KVH) == core)
        def _():
            for cc in range(2):
                w_third(hop, cc).wait_send()
                w_fourth(hop, cc).wait_send()

    vg_copy.wait_recv()
    vg_ref[0] = (half_of_images(core) + vg_recv[...].astype(F32)).astype(BF16)

    @pl.when(kind_here != core)
    def _():
        link(ysend.at[0, 0], yrecv.at[0], YS, partner).wait_recv()
        yown[...] = yrecv[0].astype(F32)

    grad = yown[...]
    for k in near_first(NY):
        link(ysend.at[0, 0], yrecv.at[k], YS + k, partner).wait_recv()
        grad = grad + yrecv[k].astype(F32)
    wg_ref[...] = grad
    vg_copy.wait_send()
    for h in range(KVH):
        for cc in range(2):
            @pl.when((core * KVH + h != t) | (core != cc))
            def _():
                y_copy(h, cc).wait_send()


def write(*refs):
    sources, targets, sem = refs[:3], refs[3:6], refs[6]
    copies = [
        pltpu.make_async_copy(src, dst, sem.at[n])
        for n, (src, dst) in enumerate(zip(sources, targets))
    ]
    for copy in copies:
        copy.start()
    for copy in copies:
        copy.wait()


def local(queries, out_grad, vision, w_kv, links, img_count):
    rows, width = queries.shape
    hbm = pl.BlockSpec(memory_space=pltpu.HBM)
    vmem = pl.BlockSpec(memory_space=pltpu.VMEM)
    sums = [
        pltpu.VMEM((NX, TOK, HD), BF16),
        pltpu.VMEM((NX, TOK, HD), BF16),
        pltpu.VMEM((TOK, HD), F32),
        pltpu.VMEM((TOK, HD), BF16),
        pltpu.VMEM((NZ, PIECE, HD), BF16),
        pltpu.VMEM((2 * KVH, TOK, HD), BF16),
    ]
    link_slots = jnp.swapaxes(links, 1, 2)
    out_shape = (
        pltpu.VMEM(queries.shape, BF16),
        pltpu.VMEM(vision.shape, BF16),
        pltpu.VMEM(w_kv.shape, F32),
    )
    results = pl.pallas_call(
        body,
        out_shape=out_shape,
        in_specs=[hbm] * 6,
        out_specs=(vmem, vmem, vmem),
        scratch_shapes=[
            pltpu.VMEM((rows, width), BF16),
            pltpu.VMEM((rows, width), BF16),
            pltpu.VMEM((2, TOK, HD), BF16),
            pltpu.VMEM(link_slots.shape, jnp.int32),
            pltpu.VMEM((1, 1), jnp.int32),
            pltpu.VMEM((TOK, HD), F32),
            pltpu.VMEM((2 * HD, TOK), BF16),
            pltpu.VMEM((KVH, 2 * HD, HD), BF16),
            pltpu.VMEM((TOK, HD), BF16),
            pltpu.VMEM((TOK, HD), BF16),
            pltpu.VMEM((KVH, TOK, GROUP * HD), BF16),
            pltpu.VMEM((KVH, 2, TOK, HD), F32),
            pltpu.VMEM((TOK, 2 * HD), F32),
            *sums,
            pltpu.VMEM((KVH, TOK, HD), BF16),
            pltpu.VMEM((KVH, TOK, HD), BF16),
            *sums,
            pltpu.VMEM((NZ, PIECE, HD), BF16),
            pltpu.VMEM((KVH, 2, HD, HD), BF16),
            pltpu.VMEM((NY, HD, HD), BF16),
            pltpu.VMEM((HD, HD), F32),
            pltpu.SemaphoreType.DMA((SEMS,)),
            pltpu.SemaphoreType.DMA((SEMS,)),
            pltpu.SemaphoreType.DMA((6,)),
        ],
        compiler_params=pltpu.CompilerParams(
            collective_id=0, has_side_effects=True, vmem_limit_bytes=40 * 1024 * 1024
        ),
    )(*[
        pltpu.with_memory_space_constraint(a, pltpu.HBM)
        for a in (queries, out_grad, vision, w_kv, link_slots)
    ], img_count.reshape(1, 1))
    return pl.pallas_call(
        write,
        out_shape=tuple(jax.ShapeDtypeStruct(r.shape, r.dtype) for r in results),
        in_specs=[vmem] * 3,
        out_specs=(hbm,) * 3,
        scratch_shapes=[pltpu.SemaphoreType.DMA((3,))],
        compiler_params=pltpu.CompilerParams(vmem_limit_bytes=4 * 1024 * 1024),
    )(*[pltpu.with_memory_space_constraint(a, pltpu.VMEM) for a in results])


def solution(mesh):
    in_specs = (
        P(("txt", "vis"), None),
        P(("txt", "vis"), None),
        P("txt", None, "vis"),
        P("vis", "txt"),
        P("txt", None, None),
        P("txt"),
    )
    out_specs = (P(("txt", "vis"), None), P("txt", None, "vis"), P("vis", "txt"))
    return jax.shard_map(local, mesh=mesh, in_specs=in_specs, out_specs=out_specs, check_vma=False)
```
